256 devices in a mesh: row: 32 (over x_hi, z, core), col: 8 (over y, x_lo).
Axes of the slice: x: 4 (x_hi: 2, x_lo: 2; x = x_hi * 2 + x_lo), y: 4, z: 8, core: 2. Of those that a mesh axis runs over, the one named last changes fastest.
Arguments:
- features: bfloat16 [65536, 128], P(('col', 'row')), may hold values from -6 to 6
- weight: bfloat16 [128, 256], replicated, may hold values from -0.5 to 0.5
- bias: float32 [256], replicated, may hold values from -3 to 3
- tile_values: bfloat16 [32, 8, 128, 128, 128], P('row', 'col'), may hold values from -0.1875 to 0.1875
- tile_row: int32 [32, 8, 128], P('row', 'col'), may hold values from 0 to 15
- tile_col: int32 [32, 8, 128], P('row', 'col'), may hold values from 0 to 63
- tile_count: int32 [32, 8], P('row', 'col'), may hold values from 1 to 128, as said below
- cotangent: bfloat16 [65536, 256], P(('row', 'col')), may hold values from -6 to 6
Outputs:
- output: bfloat16 [65536, 256], P(('row', 'col'))
- grad_features: bfloat16 [65536, 128], P(('col', 'row'))
- grad_weight: float32 [128, 256], replicated
- grad_bias: float32 [256], replicated
The draws below stay inside these ranges and needn't reach their ends.
Inputs may be any that keep to these rules, and one draw needn't show every extreme that they name: Slots from tile_count on are ignored; some device has 128 live slots and some has 1. A device may list a tile more than once; the entries then add.
All inputs are finite; a program needn't handle non-finite values.
Results may differ from the reference program's by a relative error of at most 0.02.
Values may be sent and summed in bfloat16 or wider, within the bound.
A program may use at most 64 MiB of HBM per device.

```python
import jax
import jax.numpy as jnp
from jax import lax

F = 128
H = 256
TILE = 128
NODES_DEV = 256
CAP = 128
NODES = 65536
TILE_ROWS = 16
TILE_COLS = 64
N_ROW = 32
N_COL = 8


def draw_tile_count(key, part):
    key = jax.random.fold_in(key, 7)
    key_turn, key_pick = jax.random.split(key)
    total_devices = N_ROW * N_COL
    level = jax.random.randint(key_turn, (total_devices,), 0, 64)
    counts = jnp.maximum(1, CAP // 3 * level * level // 3969).astype(jnp.int32)
    order = jax.random.permutation(key_pick, total_devices)
    counts = counts.at[order[0]].set(CAP)
    counts = counts.at[order[1]].set(1)
    return counts.reshape(N_ROW, N_COL).astype(jnp.int32)


def touch_ends(entries, stream_key, least, high):
    longest = entries.shape.index(max(entries.shape))
    spots = []
    for shift in (0, 1):
        where = [jax.random.randint(jax.random.fold_in(stream_key, axis), (), 0, length) for axis, length in enumerate(entries.shape)]
        where[longest] = (where[longest] + shift) % entries.shape[longest]
        spots.append(tuple(where))
    return entries.at[spots[0]].set(least).at[spots[1]].set(high)


def steps_of(stream_key, shape, cuts, least, largest):
    level = 1.0
    for position, shards_of in cuts:
        heights = jax.random.uniform(jax.random.fold_in(jax.random.fold_in(stream_key, 6), position), (shards_of,), jnp.float32, least / len(cuts), largest / len(cuts))
        level = level * jnp.repeat(jnp.exp(heights), shape[position] // shards_of).reshape((-1,) + (1,) * (len(shape) - 1 - position))
    return level


def bell_draw(own_key, shape, width, most, cuts=(), kind=jnp.bfloat16):
    result = width * jax.random.normal(own_key, shape, jnp.float32)
    if cuts:
        result = result * steps_of(own_key, shape, cuts, -0.22, 0.18)
    return jnp.clip(result, -most, most).astype(kind)


def setup_inputs(seed: int = 0) -> dict:
    splits = jax.random.split(jax.random.key(seed), 9)
    return {
        "features": bell_draw(splits[0], (NODES, F), 1.0, 6.0, ((0, 256),)),
        "weight": bell_draw(splits[1], (F, H), F ** -0.5, 0.5),
        "bias": bell_draw(splits[2], (H,), 0.5, 3.0, (), jnp.float32),
        "tile_values": bell_draw(splits[3], (N_ROW, N_COL, CAP, TILE, TILE), (max(128, CAP * 16384 // (9 * NODES_DEV))) ** -0.5, 0.1875, ((0, 32), (1, 8))),
        "tile_row": touch_ends(jax.random.randint(splits[4], (N_ROW, N_COL, CAP), 0, TILE_ROWS), jax.random.fold_in(splits[4], 1), 0, TILE_ROWS - 1).astype(jnp.int32),
        "tile_col": touch_ends(jax.random.randint(splits[5], (N_ROW, N_COL, CAP), 0, TILE_COLS), jax.random.fold_in(splits[5], 1), 0, TILE_COLS - 1).astype(jnp.int32),
        "tile_count": draw_tile_count(jax.random.fold_in(splits[8], 71), 0),
        "cotangent": bell_draw(splits[7], (NODES, H), 1.0, 6.0, ((0, 256),)),
    }


def slope(pre):
    sig = jax.nn.sigmoid(pre)
    return sig * (1.0 + pre * (1.0 - sig))


def reference(features, weight, bias, tile_values, tile_row, tile_col, tile_count, cotangent):
    devices_all = N_ROW * N_COL
    tiles = tile_values.reshape(devices_all, CAP, TILE, TILE)
    global_rows = (jnp.arange(N_ROW, dtype=jnp.int32)[:, None, None] * TILE_ROWS + tile_row).reshape(devices_all, CAP).astype(jnp.int32)
    global_cols = (jnp.arange(N_COL, dtype=jnp.int32)[None, :, None] * TILE_COLS + tile_col).reshape(devices_all, CAP).astype(jnp.int32)
    live = (jnp.arange(CAP, dtype=jnp.int32)[None, None, :] < tile_count[:, :, None]).reshape(devices_all, CAP)
    nodes_total = features.shape[0]
    values = jnp.dot(features, weight, preferred_element_type=jnp.float32)
    value_blocks = values.reshape(-1, TILE, H)

    def forward_step(total, item):
        tiles_here, rows_here, cols_here, live_here = item
        pieces = value_blocks[cols_here]
        contrib = jnp.einsum("kij,kjh->kih", tiles_here.astype(jnp.float32), pieces, precision=lax.Precision.HIGHEST)
        contrib = jnp.where(live_here[:, None, None], contrib, jnp.zeros_like(contrib))
        return total.at[rows_here].add(contrib), None

    summed, _ = lax.scan(forward_step, jnp.zeros((nodes_total // TILE, TILE, H), jnp.float32), (tiles, global_rows, global_cols, live))
    pre = summed.reshape(nodes_total, H) + bias.astype(jnp.float32)
    output = jax.nn.silu(pre).astype(jnp.bfloat16)
    grad_pre = (cotangent.astype(jnp.float32) * slope(pre)).astype(jnp.bfloat16)
    grad_blocks = grad_pre.astype(jnp.float32).reshape(-1, TILE, H)

    def backward_step(total, item):
        tiles_here, rows_here, cols_here, live_here = item
        pieces = grad_blocks[rows_here]
        contrib = jnp.einsum("kij,kih->kjh", tiles_here.astype(jnp.float32), pieces, precision=lax.Precision.HIGHEST)
        contrib = jnp.where(live_here[:, None, None], contrib, jnp.zeros_like(contrib))
        return total.at[cols_here].add(contrib), None

    grad_sum, _ = lax.scan(backward_step, jnp.zeros((nodes_total // TILE, TILE, H), jnp.float32), (tiles, global_rows, global_cols, live))
    grad_values = grad_sum.reshape(nodes_total, H)
    weight_full = weight.astype(jnp.float32)
    grad_features = jnp.dot(grad_values, weight_full.T, precision=lax.Precision.HIGHEST).astype(jnp.bfloat16)
    factor = nodes_total ** -0.5
    grad_weight = jnp.dot(features.astype(jnp.float32).T, grad_values, precision=lax.Precision.HIGHEST) * factor
    grad_bias = jnp.sum(grad_pre.astype(jnp.float32), axis=0) * factor
    return output, grad_features, grad_weight, grad_bias
```

```python
import functools
import math

import jax
import jax.numpy as jnp
from jax import lax
from jax.experimental import pallas as pl
from jax.experimental.pallas import tpu as pltpu
from jax.sharding import PartitionSpec as P

F32 = jnp.float32
BF16 = jnp.bfloat16
SIDE = 128
UNROLL = 8


def sort_plan(key, other, live, meta, base):
    shape = (SIDE, SIDE)
    lane = lax.broadcasted_iota(jnp.int32, shape, 1)
    sub = lax.broadcasted_iota(jnp.int32, shape, 0)
    key_l = jnp.broadcast_to(jnp.where(live, key, SIDE), shape)
    key_s = key_l.T
    other_s = jnp.broadcast_to(other, shape).T
    less = (key_l < key_s) | ((key_l == key_s) & (lane < sub))
    rank = jnp.sum(less.astype(jnp.int32), axis=1, keepdims=True)
    same = (key_l == key_s) & (lane < sub)
    keep = jnp.minimum(jnp.sum(same.astype(jnp.int32), axis=1, keepdims=True), 1)
    hot = (rank == lane).astype(jnp.int32)
    slot = jnp.sum(hot * sub, axis=0, keepdims=True)
    partner = jnp.sum(hot * other_s, axis=0, keepdims=True)
    kept = jnp.sum(hot * keep, axis=0, keepdims=True)
    upto = jnp.sum((key_s <= lane).astype(jnp.int32), axis=0, keepdims=True)
    here = jnp.sum((key_s == lane).astype(jnp.int32), axis=0, keepdims=True)
    meta[base : base + 1, :] = slot
    meta[base + 1 : base + 2, :] = partner
    meta[base + 2 : base + 3, :] = kept
    meta[base + 3 : base + 4, :] = jnp.maximum(upto - 1, 0)
    meta[base + 4 : base + 5, :] = jnp.minimum(here, 1)


def kernel(
    n_row,
    n_col,
    scale,
    x_ref,
    w_ref,
    b_ref,
    tiles_hbm,
    trow_ref,
    tcol_ref,
    count_ref,
    ct_hbm,
    out_ref,
    gf_ref,
    gw_ref,
    gb_ref,
    panel,
    tiles,
    ct,
    meta_v,
    meta,
    runs,
    rs_send,
    rs_recv,
    grads,
    dw_send,
    dw_recv,
    sib_send,
    sib_recv,
    ring_send,
    ring_recv,
    x_send,
    x_recv,
    d2_send,
    d2_recv,
    d3_send,
    d3_recv,
    local_sem,
    ag_ss,
    ag_rs,
    sib_ss,
    sib_rs,
    col_ss,
    col_rs,
    sr_ss,
    sr_rs,
    ring_ss,
    ring_rs,
    xx_ss,
    xx_rs,
    d2_ss,
    d2_rs,
):
    nz = n_row // 4
    half = nz // 2
    cap = tiles_hbm.shape[0]
    chunk = gw_ref.shape[0] // n_col
    row = lax.axis_index("row")
    col = lax.axis_index("col")
    core = row % 2
    z = (row // 2) % nz
    xh = row // (2 * nz)

    def rid(a, dz, other=0):
        xx = xh if a == 0 else 1 - xh
        kk = core if other == 0 else 1 - core
        return (xx * nz + (z + dz + nz) % nz) * 2 + kk

    def pair(index):
        return pl.ds(2 * index, 2)

    def send(src, dst, ss, rs, to_row=None, to_col=None):
        return pltpu.make_async_remote_copy(
            src_ref=src,
            dst_ref=dst,
            send_sem=ss,
            recv_sem=rs,
            device_id={
                "row": row if to_row is None else to_row,
                "col": col if to_col is None else to_col,
            },
            device_id_type=pl.DeviceIdType.MESH,
        )

    started = []

    def go(copy):
        copy.start()
        started.append(copy)

    sibling = rid(0, 0, 1)
    across = rid(1, 0)
    right = rid(0, 1)
    left = rid(0, -1)
    flips = []
    step = 1
    while step < nz:
        flips.append(rid(0, step * (1 - 2 * ((z // step) % 2))))
        step *= 2
    peers = [(col + j) % n_col for j in range(1, n_col)]

    load_x = pltpu.make_async_copy(x_ref, panel.at[pair(row)], local_sem.at[0])
    load_t = pltpu.make_async_copy(tiles_hbm, tiles, local_sem.at[1])
    load_c = pltpu.make_async_copy(ct_hbm, ct, local_sem.at[2])
    load_x.start()
    load_t.start()
    load_c.start()

    barrier = pltpu.get_barrier_semaphore()
    greet = [sibling, across, right, left] + flips[1:]
    for other in greet:
        pl.semaphore_signal(
            barrier, inc=1, device_id={"row": other, "col": col},
            device_id_type=pl.DeviceIdType.MESH,
        )
    for other in peers:
        pl.semaphore_signal(
            barrier, inc=1, device_id={"row": row, "col": other},
            device_id_type=pl.DeviceIdType.MESH,
        )
    pl.semaphore_wait(barrier, len(greet) + len(peers))

    def ag(src, blk, part, kind, to):
        dst = panel.at[pair(blk)] if part is None else panel.at[pl.ds(2 * blk + part, 1)]
        return send(src, dst, ag_ss.at[kind], ag_rs.at[kind], to)

    def kind(way, a, d):
        return 1 + (way * 2 + a) * half + d - 1

    def part_of(way, d):
        return None if d < half else way

    def view(blk, part):
        return panel.at[pair(blk)] if part is None else panel.at[pl.ds(2 * blk + part, 1)]

    def to_sibling(src, a, dz):
        k = a * nz + dz % nz
        return send(src, panel.at[pair(rid(a, dz))], sib_ss.at[k], sib_rs.at[k], sibling)

    go(ag(x_ref, row, None, kind(0, 0, 1), right))
    go(ag(x_ref, row, None, kind(1, 0, 1), left))
    go(ag(x_ref, row, None, 0, across))
    go(to_sibling(x_ref, 0, 0))

    lane1 = lax.broadcasted_iota(jnp.int32, (1, SIDE), 1)
    live = lane1 < count_ref[0, 0]
    sort_plan(trow_ref[...], tcol_ref[...], live, meta_v, 0)
    sort_plan(tcol_ref[...], trow_ref[...], live, meta_v, 5)
    load_m = pltpu.make_async_copy(meta_v, meta, local_sem.at[3])
    load_m.start()

    blk = rid(1, 0)
    ag(panel.at[pair(blk)], blk, None, 0, across).wait_recv()
    go(ag(panel.at[pair(blk)], blk, None, kind(0, 1, 1), right))
    go(ag(panel.at[pair(blk)], blk, None, kind(1, 1, 1), left))
    go(to_sibling(panel.at[pair(blk)], 1, 0))
    for d in range(1, half + 1):
        for a in (0, 1):
            for way in (0, 1):
                blk = rid(a, -d if way == 0 else d)
                part = part_of(way, d)
                ag(view(blk, part), blk, part, kind(way, a, d), left).wait_recv()
                if d < half:
                    part = part_of(way, d + 1)
                    onward = right if way == 0 else left
                    go(ag(view(blk, part), blk, part, kind(way, a, d + 1), onward))
                    go(to_sibling(panel.at[pair(blk)], a, -d if way == 0 else d))
                elif way == 1:
                    go(to_sibling(panel.at[pair(blk)], a, d))
    for dz in [0] + [s * d for d in range(1, half) for s in (1, -1)] + [half]:
        for a in (0, 1):
            k = a * nz + dz % nz
            dst = panel.at[pair(rid(a, dz, 1))]
            send(dst, dst, sib_ss.at[k], sib_rs.at[k], sibling).wait_recv()
    load_x.wait()
    load_t.wait()
    load_m.wait()

    def products(base, forward):
        def turn(i, acc):
            for u in range(UNROLL):
                s = i * UNROLL + u
                tile = tiles[meta[base, s]]
                if forward:
                    prod = jnp.dot(tile, panel[meta[base + 1, s]], preferred_element_type=F32)
                else:
                    prod = jnp.dot(grads[meta[base + 1, s]], tile, preferred_element_type=F32)
                acc = acc * meta[base + 2, s].astype(F32) + prod
                runs[s] = acc
            return acc

        lax.fori_loop(0, cap // UNROLL, turn, jnp.zeros((SIDE, SIDE), F32))

    def total(base, index):
        return runs[meta[base + 3, index]] * meta[base + 4, index].astype(F32)

    products(0, True)

    for j in range(1, n_col):
        to = peers[j - 1]
        for t in (0, 1):
            rs_send[2 * to + t] = total(0, 2 * to + t).astype(BF16)
        go(send(rs_send.at[pair(to)], rs_recv.at[pair(col)], col_ss.at[j], col_rs.at[j], None, to))
    agg = [total(0, 2 * col + t) for t in (0, 1)]
    load_c.wait()
    for j in range(1, n_col):
        src = (col - j + n_col) % n_col
        send(rs_send.at[pair(src)], rs_recv.at[pair(src)], col_ss.at[j], col_rs.at[j], None, src).wait_recv()
        for t in (0, 1):
            agg[t] = agg[t] + rs_recv[2 * src + t].astype(F32)

    w = w_ref[...]
    gps = []
    outs = []
    for t in (0, 1):
        hi = agg[t].astype(BF16)
        lo = (agg[t] - hi.astype(F32)).astype(BF16)
        pre = jnp.dot(hi, w, preferred_element_type=F32) + jnp.dot(lo, w, preferred_element_type=F32)
        pre = pre + b_ref[...]
        sig = jax.nn.sigmoid(pre)
        outs.append((pre * sig).astype(BF16))
        slope = sig * (1.0 + pre * (1.0 - sig))
        gp = (ct[t * SIDE : (t + 1) * SIDE, :].astype(F32) * slope).astype(BF16)
        gps.append(gp)
        back = lax.dot_general(w, gp, (((1,), (1,)), ((), ())), preferred_element_type=F32)
        grads[2 * col + t] = back.astype(BF16)
    for j in range(1, n_col):
        k = n_col + j
        go(send(grads.at[pair(col)], grads.at[pair(col)], col_ss.at[k], col_rs.at[k], None, peers[j - 1]))

    for t in (0, 1):
        out_ref[t * SIDE : (t + 1) * SIDE, :] = outs[t]
    bias = jnp.sum(gps[0].astype(F32), axis=0, keepdims=True) + jnp.sum(gps[1].astype(F32), axis=0, keepdims=True)
    dw = jnp.zeros(gw_ref.shape, F32)
    for t in (0, 1):
        turned = agg[t].T
        hi = turned.astype(BF16)
        lo = (turned - hi.astype(F32)).astype(BF16)
        dw = dw + jnp.dot(hi, gps[t], preferred_element_type=F32)
        dw = dw + jnp.dot(lo, gps[t], preferred_element_type=F32)
    bias8 = jnp.broadcast_to(bias, (8, bias.shape[1]))
    for c in range(n_col):
        dw_send[c, :chunk, :] = dw[c * chunk : (c + 1) * chunk, :]
        dw_send[c, chunk:, :] = bias8
    dw_recv[col] = dw_send[col]
    for j in range(1, n_col):
        k = 2 * n_col + j
        to = peers[j - 1]
        go(send(dw_send.at[to], dw_recv.at[col], col_ss.at[k], col_rs.at[k], None, to))

    for j in range(1, n_col):
        k = n_col + j
        src = (col - j + n_col) % n_col
        send(grads.at[pair(src)], grads.at[pair(src)], col_ss.at[k], col_rs.at[k], None, src).wait_recv()

    products(5, False)

    order = [half] + [s * d for d in range(half - 1, 0, -1) for s in (1, -1)] + [0]
    for dz in order:
        slot = dz % nz
        for a in (1, 0):
            for t in (0, 1):
                sib_send[slot, 2 * a + t] = total(5, 2 * rid(a, dz, 1) + t).astype(BF16)
        go(send(sib_send.at[slot], sib_recv.at[slot], sr_ss.at[slot], sr_rs.at[slot], sibling))

    for j in range(1, n_col):
        k = 2 * n_col + j
        src = (col - j + n_col) % n_col
        send(dw_send.at[src], dw_recv.at[src], col_ss.at[k], col_rs.at[k], None, src).wait_recv()
    d2_partners = [sibling] + flips + [across]
    weight_sum = [dw_recv[0]]
    for c in range(1, n_col):
        weight_sum[0] = weight_sum[0] + dw_recv[c]

    def d2_copy(i):
        return send(d2_send.at[i], d2_recv.at[i], d2_ss.at[i], d2_rs.at[i], d2_partners[i])

    def d2_start(i):
        d2_send[i] = weight_sum[0]
        go(d2_copy(i))

    def d2_finish(i):
        d2_copy(i).wait_recv()
        weight_sum[0] = d2_send[i] + d2_recv[i]

    d2_start(0)

    def comb(dz, a, t):
        return total(5, 2 * rid(a, dz) + t) + sib_recv[dz % nz, 2 * a + t].astype(F32)

    def sib_wait(dz):
        slot = dz % nz
        send(sib_send.at[slot], sib_recv.at[slot], sr_ss.at[slot], sr_rs.at[slot], sibling).wait_recv()

    def ring(way, n, a):
        k = (way * half + n) * 2 + a
        if n == 0:
            src, dst = ring_send.at[k, pl.ds(way, 1)], ring_recv.at[k, pl.ds(way, 1)]
        else:
            src, dst = ring_send.at[k], ring_recv.at[k]
        return send(src, dst, ring_ss.at[k], ring_rs.at[k], right if way == 0 else left)

    def arrived(way, n, a, t):
        return ring_recv[(way * half + n) * 2 + a, t].astype(F32)

    for n in range(half):
        dist = half - n
        for a in (1, 0):
            for way in (0, 1):
                dz = dist if way == 0 else -dist
                if a == 1 and not (n == 0 and way == 1):
                    sib_wait(dz)
                if n > 0:
                    ring(way, n - 1, a).wait_recv()
                for t in (0, 1):
                    if n == 0 and t != way:
                        continue
                    value = comb(dz, a, t)
                    if n > 1 or (n == 1 and t == way):
                        value = value + arrived(way, n - 1, a, t)
                    ring_send[(way * half + n) * 2 + a, t] = value.astype(BF16)
                go(ring(way, n, a))
        if n < len(d2_partners) - 1:
            d2_finish(n)
            d2_start(n + 1)
    for i in range(half, len(d2_partners) - 1):
        d2_finish(i)
        d2_start(i + 1)
    sib_wait(0)
    last = half - 1
    x_copy = send(x_send, x_recv, xx_ss.at[0], xx_rs.at[0], across)
    done = []
    for a in (1, 0):
        for way in (0, 1):
            ring(way, last, a).wait_recv()
        for t in (0, 1):
            value = comb(0, a, t)
            for way in (0, 1):
                if last > 0 or t == way:
                    value = value + arrived(way, last, a, t)
            if a == 1:
                x_send[t] = value.astype(BF16)
            else:
                done.append(value)
        if a == 1:
            go(x_copy)
    d2_finish(len(d2_partners) - 1)
    d3_send[...] = weight_sum[0][:chunk, :] * scale
    gb_ref[...] = weight_sum[0][chunk : chunk + 1, :] * scale
    d3_recv[col] = d3_send[...]
    for j in range(1, n_col):
        k = 3 * n_col + j
        go(send(d3_send, d3_recv.at[col], col_ss.at[k], col_rs.at[k], None, peers[j - 1]))
    x_copy.wait_recv()
    for t in (0, 1):
        value = done[t] + x_recv[t].astype(F32)
        gf_ref[t * SIDE : (t + 1) * SIDE, :] = value.T.astype(BF16)
    for j in range(1, n_col):
        k = 3 * n_col + j
        src = (col - j + n_col) % n_col
        send(d3_send, d3_recv.at[src], col_ss.at[k], col_rs.at[k], None, src).wait_recv()
    for c in range(n_col):
        gw_ref[c * chunk : (c + 1) * chunk, :] = d3_recv[c]
    for copy in started:
        copy.wait_send()


def local(n_row, n_col, features, weight, bias, tile_values, tile_row, tile_col, tile_count, cotangent):
    nodes, f = features.shape
    h = weight.shape[1]
    cap = tile_values.shape[2]
    nz = n_row // 4
    half = nz // 2
    flips = max(1, nz.bit_length() - 1)
    chunk = f // n_col
    scale = (n_row * n_col * nodes) ** (-0.5)
    pad = SIDE - tile_row.shape[-1]
    trow = jnp.pad(tile_row.reshape(1, -1), ((0, 0), (0, pad)))
    tcol = jnp.pad(tile_col.reshape(1, -1), ((0, 0), (0, pad)))
    vmem = pl.BlockSpec(memory_space=pltpu.VMEM)
    anywhere = pl.BlockSpec(memory_space=pl.ANY)
    dma = pltpu.SemaphoreType.DMA
    square = (SIDE, SIDE)
    output, gf, gw, gb = pl.pallas_call(
        functools.partial(kernel, n_row, n_col, scale),
        out_shape=(
            jax.ShapeDtypeStruct((nodes, h), BF16),
            jax.ShapeDtypeStruct((nodes, f), BF16),
            jax.ShapeDtypeStruct((f, h), F32),
            jax.ShapeDtypeStruct((1, h), F32),
        ),
        in_specs=[anywhere, vmem, vmem, anywhere, vmem, vmem, pl.BlockSpec(memory_space=pltpu.SMEM), anywhere],
        out_specs=(vmem,) * 4,
        scratch_shapes=[
            pltpu.VMEM((2 * n_row,) + square, BF16),
            pltpu.VMEM((cap,) + square, BF16),
            pltpu.VMEM((nodes, h), BF16),
            pltpu.VMEM((16, SIDE), jnp.int32),
            pltpu.SMEM((16, SIDE), jnp.int32),
            pltpu.VMEM((cap,) + square, F32),
            pltpu.VMEM((2 * n_col,) + square, BF16),
            pltpu.VMEM((2 * n_col,) + square, BF16),
            pltpu.VMEM((2 * n_col,) + square, BF16),
            pltpu.VMEM((n_col, chunk + 8, h), F32),
            pltpu.VMEM((n_col, chunk + 8, h), F32),
            pltpu.VMEM((nz, 4) + square, BF16),
            pltpu.VMEM((nz, 4) + square, BF16),
            pltpu.VMEM((4 * half, 2) + square, BF16),
            pltpu.VMEM((4 * half, 2) + square, BF16),
            pltpu.VMEM((2,) + square, BF16),
            pltpu.VMEM((2,) + square, BF16),
            pltpu.VMEM((flips + 2, chunk + 8, h), F32),
            pltpu.VMEM((flips + 2, chunk + 8, h), F32),
            pltpu.VMEM((chunk, h), F32),
            pltpu.VMEM((n_col, chunk, h), F32),
            dma((4,)),
            dma((1 + 4 * half,)),
            dma((1 + 4 * half,)),
            dma((2 * nz,)),
            dma((2 * nz,)),
            dma((4 * n_col,)),
            dma((4 * n_col,)),
            dma((nz,)),
            dma((nz,)),
            dma((4 * half,)),
            dma((4 * half,)),
            dma((1,)),
            dma((1,)),
            dma((flips + 2,)),
            dma((flips + 2,)),
        ],
        compiler_params=pltpu.CompilerParams(
            collective_id=0, has_side_effects=True, vmem_limit_bytes=48 * 1024 * 1024
        ),
    )(
        features.reshape(2, SIDE, f),
        weight,
        bias.reshape(1, h),
        tile_values.reshape(tile_values.shape[2:]),
        trow,
        tcol,
        tile_count,
        cotangent,
    )
    return output, gf, gw, gb.reshape(h)


def solution(mesh):
    placed = (
        P(("col", "row"), None),
        P(),
        P(),
        P("row", "col", None, None, None),
        P("row", "col", None),
        P("row", "col", None),
        P("row", "col"),
        P(("row", "col"), None),
    )
    return jax.shard_map(
        functools.partial(local, mesh.shape["row"], mesh.shape["col"]),
        mesh=mesh,
        in_specs=placed,
        out_specs=(P(("row", "col"), None), P(("col", "row"), None), P(), P()),
        check_vma=False,
    )
```

```python
import functools

import jax
import jax.numpy as jnp
from jax import lax
from jax.experimental import pallas as pl
from jax.experimental.pallas import tpu as pltpu
from jax.sharding import PartitionSpec as P

F32 = jnp.float32
BF16 = jnp.bfloat16
SIDE = 128
UNROLL = 8


def sort_plan(key, other, live, meta, base):
    shape = (SIDE, SIDE)
    lane = lax.broadcasted_iota(jnp.int32, shape, 1)
    sub = lax.broadcasted_iota(jnp.int32, shape, 0)
    key_l = jnp.broadcast_to(jnp.where(live, key, SIDE), shape)
    key_s = key_l.T
    other_s = jnp.broadcast_to(other, shape).T
    less = (key_l < key_s) | ((key_l == key_s) & (lane < sub))
    rank = jnp.sum(less.astype(jnp.int32), axis=1, keepdims=True)
    same = (key_l == key_s) & (lane < sub)
    keep = jnp.minimum(jnp.sum(same.astype(jnp.int32), axis=1, keepdims=True), 1)
    hot = (rank == lane).astype(jnp.int32)
    slot = jnp.sum(hot * sub, axis=0, keepdims=True)
    partner = jnp.sum(hot * other_s, axis=0, keepdims=True)
    kept = jnp.sum(hot * keep, axis=0, keepdims=True)
    upto = jnp.sum((key_s <= lane).astype(jnp.int32), axis=0, keepdims=True)
    here = jnp.sum((key_s == lane).astype(jnp.int32), axis=0, keepdims=True)
    meta[base : base + 1, :] = slot
    meta[base + 1 : base + 2, :] = partner
    meta[base + 2 : base + 3, :] = kept
    meta[base + 3 : base + 4, :] = jnp.maximum(upto - 1, 0)
    meta[base + 4 : base + 5, :] = jnp.minimum(here, 1)


def kernel(
    n_row,
    n_col,
    scale,
    x_ref,
    w_hbm,
    b_hbm,
    tiles_hbm,
    trow_hbm,
    tcol_hbm,
    count_ref,
    ct_hbm,
    out_ref,
    gf_ref,
    gw_ref,
    gb_ref,
    w_ref,
    b_ref,
    trow_ref,
    tcol_ref,
    panel,
    tiles,
    ct,
    meta_v,
    meta,
    runs,
    rs_send,
    rs_recv,
    grads,
    sib_send,
    sib_recv,
    ring_send,
    ring_recv,
    wz_send,
    wz_recv,
    wc_send,
    wc_recv,
    wx_send,
    wx_recv,
    wg_send,
    wg_recv,
    local_sem,
    ag_ss,
    ag_rs,
    sib_ss,
    sib_rs,
    col_ss,
    col_rs,
    sr_ss,
    sr_rs,
    ring_ss,
    ring_rs,
    w_ss,
    w_rs,
):
    nz = n_row // 4
    ny = n_col // 2
    cap = tiles_hbm.shape[0]
    chunk = gw_ref.shape[0] // nz
    row = lax.axis_index("row")
    col = lax.axis_index("col")
    core = row % 2
    z = (row // 2) % nz
    xh = row // (2 * nz)
    y = col // 2
    xl = col % 2

    def rid(a, dz, other=0):
        xx = xh if a == 0 else 1 - xh
        kk = core if other == 0 else 1 - core
        return (xx * nz + (z + dz + nz) % nz) * 2 + kk

    def cid(dy, dx):
        return ((y + dy + ny) % ny) * 2 + (xl + dx) % 2

    def pair(index):
        return pl.ds(2 * index, 2)

    def send(src, dst, ss, rs, to_row=None, to_col=None):
        return pltpu.make_async_remote_copy(
            src_ref=src,
            dst_ref=dst,
            send_sem=ss,
            recv_sem=rs,
            device_id={
                "row": row if to_row is None else to_row,
                "col": col if to_col is None else to_col,
            },
            device_id_type=pl.DeviceIdType.MESH,
        )

    started = []

    def go(copy):
        copy.start()
        started.append(copy)

    sibling = rid(0, 0, 1)
    across = rid(1, 0)
    shifts = sorted(
        ((dy, dx) for dy in range(ny) for dx in range(2) if dy or dx),
        key=lambda p: -(min(p[0], ny - p[0]) + p[1]),
    )

    loads = [
        pltpu.make_async_copy(src, dst, local_sem.at[i])
        for i, (src, dst) in enumerate(
            (
                (trow_hbm, trow_ref),
                (tcol_hbm, tcol_ref),
                (x_ref, panel.at[pair(row)]),
                (w_hbm, w_ref),
                (b_hbm, b_ref),
                (ct_hbm, ct),
                (tiles_hbm, tiles),
            )
        )
    ]
    for load in loads:
        load.start()

    barrier = pltpu.get_barrier_semaphore()
    greet = [sibling, across, rid(1, 0, 1)] + [rid(0, d) for d in range(1, nz)]
    for other in greet:
        pl.semaphore_signal(
            barrier, inc=1, device_id={"row": other, "col": col},
            device_id_type=pl.DeviceIdType.MESH,
        )
    for shift in shifts:
        pl.semaphore_signal(
            barrier, inc=1, device_id={"row": row, "col": cid(*shift)},
            device_id_type=pl.DeviceIdType.MESH,
        )
    pl.semaphore_wait(barrier, len(greet) + len(shifts))

    def ag(a, dz, t, to, src=None):
        k = (a * nz + dz % nz) * 2 + t
        if src is None:
            src = rid(a, dz)
        return send(
            x_ref.at[pl.ds(t, 1)] if to is not None and src is row else panel.at[pl.ds(2 * src + t, 1)],
            panel.at[pl.ds(2 * src + t, 1)],
            ag_ss.at[k],
            ag_rs.at[k],
            across if to is None else to,
        )

    def ag_wait(a, dz, t):
        ag(a, dz, t, None).wait_recv()

    def to_sibling(a, dz):
        k = a * nz + dz % nz
        blk = rid(a, dz)
        src = x_ref if a == 0 and dz == 0 else panel.at[pair(blk)]
        go(send(src, panel.at[pair(blk)], sib_ss.at[k], sib_rs.at[k], sibling))

    signs = (1, -1)
    for t in (0, 1):
        for e in signs:
            go(ag(0, -2 * e, t, rid(0, 2 * e), row))
        go(ag(1, 0, t, across, row))
    for t in (0, 1):
        for e in signs:
            go(ag(0, -e, t, rid(0, e), row))
    to_sibling(0, 0)

    for load in loads[:2]:
        load.wait()
    lane1 = lax.broadcasted_iota(jnp.int32, (1, SIDE), 1)
    live = lane1 < count_ref[0, 0]
    sort_plan(trow_ref[...], tcol_ref[...], live, meta_v, 0)
    sort_plan(tcol_ref[...], trow_ref[...], live, meta_v, 5)
    load_m = pltpu.make_async_copy(meta_v, meta, local_sem.at[7])
    load_m.start()

    for t in (0, 1):
        for e in signs:
            ag_wait(0, -2 * e, t)
            go(ag(1, -2 * e, t, across, rid(0, -2 * e)))
    for t in (0, 1):
        ag_wait(1, 0, t)
        for e in signs:
            go(ag(0, -3 * e, t, rid(0, e), rid(0, -2 * e)))
            go(ag(1, -e, t, rid(0, e), across))
    for t, e in enumerate(signs):
        go(ag(0, 4, t, rid(0, 2 * e), rid(0, -2 * e)))
    for e in signs:
        to_sibling(0, -2 * e)
    to_sibling(1, 0)
    for e in signs:
        for t in (0, 1):
            ag_wait(0, -e, t)
        to_sibling(0, -e)
    for t in (0, 1):
        for e in signs:
            ag_wait(1, -2 * e, t)
            if t == (0 if e == 1 else 1):
                go(ag(1, 4, t, rid(0, 2 * e), rid(1, -2 * e)))
            go(ag(1, -3 * e, t, rid(0, e), rid(1, -2 * e)))
    for e in signs:
        to_sibling(1, -2 * e)
    for a, dz in ((0, -3), (0, 3), (1, -1), (1, 1), (0, 4), (1, -3), (1, 3), (1, 4)):
        for t in (0, 1):
            ag_wait(a, dz, t)
        to_sibling(a, dz)
    for dz in (0, -2, 2, -1, 1, -3, 3, 4):
        for a in (0, 1):
            k = a * nz + dz % nz
            dst = panel.at[pair(rid(a, dz, 1))]
            send(dst, dst, sib_ss.at[k], sib_rs.at[k], sibling).wait_recv()
    for load in loads[2:]:
        load.wait()
    load_m.wait()

    def products(base, forward):
        def turn(i, acc):
            for u in range(UNROLL):
                s = i * UNROLL + u
                tile = tiles[meta[base, s]]
                if forward:
                    prod = jnp.dot(tile, panel[meta[base + 1, s]], preferred_element_type=F32)
                else:
                    prod = jnp.dot(grads[meta[base + 1, s]], tile, preferred_element_type=F32)
                acc = acc * meta[base + 2, s].astype(F32) + prod
                runs[s] = acc
            return acc

        lax.fori_loop(0, cap // UNROLL, turn, jnp.zeros((SIDE, SIDE), F32))

    def total(base, index):
        return runs[meta[base + 3, index]] * meta[base + 4, index].astype(F32)

    products(0, True)

    def cc(src, dst, k, to):
        return send(src, dst, col_ss.at[k], col_rs.at[k], None, to)

    for j, shift in enumerate(shifts):
        to = cid(*shift)
        for t in (0, 1):
            rs_send[2 * to + t] = total(0, 2 * to + t).astype(BF16)
        go(cc(rs_send.at[pair(to)], rs_recv.at[pair(col)], j, to))
    agg = [total(0, 2 * col + t) for t in (0, 1)]
    for j, (dy, dx) in reversed(list(enumerate(shifts))):
        src = cid(-dy, dx)
        cc(rs_send.at[pair(src)], rs_recv.at[pair(src)], j, src).wait_recv()
        for t in (0, 1):
            agg[t] = agg[t] + rs_recv[2 * src + t].astype(F32)

    w = w_ref[...]
    gps = []
    outs = []
    for t in (0, 1):
        hi = agg[t].astype(BF16)
        lo = (agg[t] - hi.astype(F32)).astype(BF16)
        pre = jnp.dot(hi, w, preferred_element_type=F32) + jnp.dot(lo, w, preferred_element_type=F32)
        pre = pre + b_ref[...]
        sig = jax.nn.sigmoid(pre)
        outs.append((pre * sig).astype(BF16))
        slope = sig * (1.0 + pre * (1.0 - sig))
        gp = (ct[t * SIDE : (t + 1) * SIDE, :].astype(F32) * slope).astype(BF16)
        gps.append(gp)
        back = lax.dot_general(w, gp, (((1,), (1,)), ((), ())), preferred_element_type=F32)
        grads[2 * col + t] = back.astype(BF16)
        own = grads.at[pl.ds(2 * col + t, 1)]
        for j, shift in enumerate(shifts):
            go(cc(own, own, (1 + t) * n_col + j, cid(*shift)))

    bias = jnp.sum(gps[0].astype(F32), axis=0, keepdims=True) + jnp.sum(gps[1].astype(F32), axis=0, keepdims=True)
    dw = jnp.zeros(gw_ref.shape, F32)
    for t in (0, 1):
        turned = agg[t].T
        hi = turned.astype(BF16)
        lo = (turned - hi.astype(F32)).astype(BF16)
        dw = dw + jnp.dot(hi, gps[t], preferred_element_type=F32)
        dw = dw + jnp.dot(lo, gps[t], preferred_element_type=F32)
    bias8 = jnp.broadcast_to(bias, (8, bias.shape[1]))
    for c in range(nz):
        wz_send[c, :chunk, :] = dw[c * chunk : (c + 1) * chunk, :]
        wz_send[c, chunk:, :] = bias8
    wz_recv[z] = wz_send[z]

    def wcopy(src, dst, k, to_row=None, to_col=None):
        return send(src, dst, w_ss.at[k], w_rs.at[k], to_row, to_col)

    far = sorted(range(1, nz), key=lambda d: -min(d, nz - d))
    for d in far:
        go(wcopy(wz_send.at[(z + d) % nz], wz_recv.at[z], d, rid(0, d)))
    for t in (0, 1):
        out_ref[t * SIDE : (t + 1) * SIDE, :] = outs[t]

    for t in (0, 1):
        for j, (dy, dx) in enumerate(shifts):
            src = cid(-dy, dx)
            there = grads.at[pl.ds(2 * src + t, 1)]
            cc(there, there, (1 + t) * n_col + j, src).wait_recv()

    products(5, False)

    def added(ref, n):
        value = ref[0]
        for i in range(1, n):
            value = value + ref[i]
        return value

    def over_z_done():
        for d in far:
            src = (z - d + nz) % nz
            wcopy(wz_send.at[src], wz_recv.at[src], d, rid(0, -d)).wait_recv()
        value = added(wz_recv, nz)
        wc_send[...] = value
        wc_recv[col] = value
        for j, shift in enumerate(shifts):
            go(wcopy(wc_send, wc_recv.at[col], nz + j, None, cid(*shift)))

    quad = 2 * xh + core
    quads = ((1, 1), (1, 0), (0, 1))

    def over_col_done():
        for j, (dy, dx) in enumerate(shifts):
            src = cid(-dy, dx)
            wcopy(wc_send, wc_recv.at[src], nz + j, None, src).wait_recv()
        value = added(wc_recv, n_col)
        wx_send[...] = value
        wx_recv[quad] = value
        for j, (a, other) in enumerate(quads):
            go(wcopy(wx_send, wx_recv.at[quad], nz + n_col + j, rid(a, 0, other)))

    def over_quad_done():
        for j, (a, other) in enumerate(quads):
            src = 2 * (xh if a == 0 else 1 - xh) + (core if other == 0 else 1 - core)
            wcopy(wx_send, wx_recv.at[src], nz + n_col + j, rid(a, 0, other)).wait_recv()
        value = added(wx_recv, 4) * scale
        gb_ref[...] = value[chunk : chunk + 1, :]
        wg_send[...] = value[:chunk, :]
        wg_recv[z] = value[:chunk, :]
        for d in far:
            go(wcopy(wg_send, wg_recv.at[z], nz + n_col + 4 + d, rid(0, d)))

    def gathered():
        for d in far:
            src = (z - d + nz) % nz
            wcopy(wg_send, wg_recv.at[src], nz + n_col + 4 + d, rid(0, -d)).wait_recv()
        for c in range(nz):
            gw_ref[c * chunk : (c + 1) * chunk, :] = wg_recv[c]

    order = [(1, 3), (1, -3), (1, 4), (0, 3), (0, -3), (0, 4), (1, 2), (1, -2)]
    order += [(1, 1), (1, -1), (0, 1), (0, -1), (0, 2), (0, -2), (1, 0), (0, 0)]

    def sib_copy(a, dz):
        k = a * nz + dz % nz
        return send(sib_send.at[k], sib_recv.at[k], sr_ss.at[k], sr_rs.at[k], sibling)

    for a, dz in order:
        for t in (0, 1):
            sib_send[a * nz + dz % nz, t] = total(5, 2 * rid(a, dz, 1) + t).astype(BF16)
        go(sib_copy(a, dz))
    over_z_done()

    def comb(a, dz, t):
        return total(5, 2 * rid(a, dz) + t) + sib_recv[a * nz + dz % nz, t].astype(F32)

    slots = {}
    for a in (0, 1):
        for e in signs:
            for name in ("three", "four", "one"):
                slots[name, a, e] = len(slots)
    for e in signs:
        slots["cross", 0, e] = len(slots)
        slots["two", 0, e] = len(slots)
    slots["zero", 0, 1] = len(slots)

    def ring(name, a, e, t, to):
        k = slots[name, a, e]
        return send(
            ring_send.at[k, pl.ds(t, 1)],
            ring_recv.at[k, pl.ds(t, 1)],
            ring_ss.at[2 * k + t],
            ring_rs.at[2 * k + t],
            to,
        )

    def ring_go(name, a, e, t, to, value):
        ring_send[slots[name, a, e], t] = value.astype(BF16)
        go(ring(name, a, e, t, to))

    def arrived(name, a, e, t):
        ring(name, a, e, t, across).wait_recv()
        return ring_recv[slots[name, a, e], t].astype(F32)

    for a in (1, 0):
        for e in signs:
            sib_copy(a, 3 * e).wait_recv()
            for t in (0, 1):
                ring_go("three", a, e, t, rid(0, e), comb(a, 3 * e, t))
        sib_copy(a, 4).wait_recv()
        for t, e in enumerate((-1, 1)):
            ring_go("four", a, e, t, rid(0, 2 * e), comb(a, 4, t))
    for a in (1, 0):
        for e in signs:
            sib_copy(a, e).wait_recv()
            for t in (0, 1):
                ring_go("one", a, e, t, rid(0, e), comb(a, e, t))

    def near(a, e, t):
        value = comb(a, 2 * e, t) + arrived("three", a, e, t)
        if t == (0 if e == -1 else 1):
            value = value + arrived("four", a, e, t)
        return value

    for e in signs:
        sib_copy(1, 2 * e).wait_recv()
    for t in (0, 1):
        for e in signs:
            ring_go("cross", 0, e, t, across, near(1, e, t))
    over_col_done()
    sib_copy(1, 0).wait_recv()
    for t in (0, 1):
        value = comb(1, 0, t) + arrived("one", 1, 1, t) + arrived("one", 1, -1, t)
        ring_go("zero", 0, 1, t, across, value)
    for e in signs:
        sib_copy(0, 2 * e).wait_recv()
    for t in (0, 1):
        for e in signs:
            value = near(0, e, t) + arrived("cross", 0, e, t)
            ring_go("two", 0, e, t, rid(0, 2 * e), value)
    over_quad_done()
    sib_copy(0, 0).wait_recv()
    for t in (0, 1):
        value = comb(0, 0, t)
        for e in signs:
            value = value + arrived("one", 0, e, t)
        value = value + arrived("zero", 0, 1, t)
        for e in signs:
            value = value + arrived("two", 0, e, t)
        gf_ref[t * SIDE : (t + 1) * SIDE, :] = value.T.astype(BF16)
    gathered()
    for copy in started:
        copy.wait_send()


def write_out(*refs):
    copies = [pltpu.make_async_copy(refs[i], refs[4 + i], refs[8].at[i]) for i in range(4)]
    for copy in copies:
        copy.start()
    for copy in copies:
        copy.wait()


def local(n_row, n_col, features, weight, bias, tile_values, tile_row, tile_col, tile_count, cotangent):
    nodes, f = features.shape
    h = weight.shape[1]
    cap = tile_values.shape[2]
    nz = n_row // 4
    chunk = f // nz
    scale = (n_row * n_col * nodes) ** (-0.5)
    pad = SIDE - tile_row.shape[-1]
    trow = jnp.pad(tile_row.reshape(1, -1), ((0, 0), (0, pad)))
    tcol = jnp.pad(tile_col.reshape(1, -1), ((0, 0), (0, pad)))
    vmem = pl.BlockSpec(memory_space=pltpu.VMEM)
    hbm = pl.BlockSpec(memory_space=pltpu.HBM)
    dma = pltpu.SemaphoreType.DMA
    square = (SIDE, SIDE)
    output, gf, gw, gb = pl.pallas_call(
        functools.partial(kernel, n_row, n_col, scale),
        out_shape=(
            jax.ShapeDtypeStruct((nodes, h), BF16),
            jax.ShapeDtypeStruct((nodes, f), BF16),
            jax.ShapeDtypeStruct((f, h), F32),
            jax.ShapeDtypeStruct((1, h), F32),
        ),
        in_specs=[hbm] * 6 + [pl.BlockSpec(memory_space=pltpu.SMEM), hbm],
        out_specs=(vmem,) * 4,
        scratch_shapes=[
            pltpu.VMEM((f, h), BF16),
            pltpu.VMEM((1, h), F32),
            pltpu.VMEM((1, SIDE), jnp.int32),
            pltpu.VMEM((1, SIDE), jnp.int32),
            pltpu.VMEM((2 * n_row,) + square, BF16),
            pltpu.VMEM((cap,) + square, BF16),
            pltpu.VMEM((nodes, h), BF16),
            pltpu.VMEM((16, SIDE), jnp.int32),
            pltpu.SMEM((16, SIDE), jnp.int32),
            pltpu.VMEM((cap,) + square, F32),
            pltpu.VMEM((2 * n_col,) + square, BF16),
            pltpu.VMEM((2 * n_col,) + square, BF16),
            pltpu.VMEM((2 * n_col,) + square, BF16),
            pltpu.VMEM((2 * nz, 2) + square, BF16),
            pltpu.VMEM((2 * nz, 2) + square, BF16),
            pltpu.VMEM((17, 2) + square, BF16),
            pltpu.VMEM((17, 2) + square, BF16),
            pltpu.VMEM((nz, chunk + 8, h), F32),
            pltpu.VMEM((nz, chunk + 8, h), F32),
            pltpu.VMEM((chunk + 8, h), F32),
            pltpu.VMEM((n_col, chunk + 8, h), F32),
            pltpu.VMEM((chunk + 8, h), F32),
            pltpu.VMEM((4, chunk + 8, h), F32),
            pltpu.VMEM((chunk, h), F32),
            pltpu.VMEM((nz, chunk, h), F32),
            dma((8,)),
            dma((4 * nz,)),
            dma((4 * nz,)),
            dma((2 * nz,)),
            dma((2 * nz,)),
            dma((3 * n_col,)),
            dma((3 * n_col,)),
            dma((2 * nz,)),
            dma((2 * nz,)),
            dma((34,)),
            dma((34,)),
            dma((2 * nz + n_col + 4,)),
            dma((2 * nz + n_col + 4,)),
        ],
        compiler_params=pltpu.CompilerParams(
            collective_id=0, has_side_effects=True, vmem_limit_bytes=48 * 1024 * 1024
        ),
    )(
        *(
            pltpu.with_memory_space_constraint(operand, pltpu.HBM)
            for operand in (
                features.reshape(2, SIDE, f),
                weight,
                bias.reshape(1, h),
                tile_values.reshape(tile_values.shape[2:]),
                trow,
                tcol,
            )
        ),
        tile_count,
        pltpu.with_memory_space_constraint(cotangent, pltpu.HBM),
    )
    results = (output, gf, gw, gb)
    output, gf, gw, gb = pl.pallas_call(
        write_out,
        out_shape=tuple(jax.ShapeDtypeStruct(a.shape, a.dtype) for a in results),
        in_specs=[pl.BlockSpec(memory_space=pl.ANY)] * 4,
        out_specs=(hbm,) * 4,
        scratch_shapes=[dma((4,))],
        compiler_params=pltpu.CompilerParams(vmem_limit_bytes=1024 * 1024),
    )(*(pltpu.with_memory_space_constraint(a, pltpu.VMEM) for a in results))
    return output, gf, gw, gb.reshape(h)


def solution(mesh):
    placed = (
        P(("col", "row"), None),
        P(),
        P(),
        P("row", "col", None, None, None),
        P("row", "col", None),
        P("row", "col", None),
        P("row", "col"),
        P(("row", "col"), None),
    )
    return jax.shard_map(
        functools.partial(local, mesh.shape["row"], mesh.shape["col"]),
        mesh=mesh,
        in_specs=placed,
        out_specs=(P(("row", "col"), None), P(("col", "row"), None), P(), P()),
        check_vma=False,
    )
```

```python
import functools

import jax
import jax.numpy as jnp
from jax import lax
from jax.experimental import pallas as pl
from jax.experimental.pallas import tpu as pltpu
from jax.sharding import PartitionSpec as P

F32 = jnp.float32
BF16 = jnp.bfloat16
SIDE = 128
UNROLL = 8


def sort_plan(key, other, live, meta, base):
    shape = (SIDE, SIDE)
    lane = lax.broadcasted_iota(jnp.int32, shape, 1)
    sub = lax.broadcasted_iota(jnp.int32, shape, 0)
    key_l = jnp.broadcast_to(jnp.where(live, key, SIDE), shape)
    key_s = key_l.T
    other_s = jnp.broadcast_to(other, shape).T
    less = (key_l < key_s) | ((key_l == key_s) & (lane < sub))
    rank = jnp.sum(less.astype(jnp.int32), axis=1, keepdims=True)
    same = (key_l == key_s) & (lane < sub)
    keep = jnp.minimum(jnp.sum(same.astype(jnp.int32), axis=1, keepdims=True), 1)
    hot = (rank == lane).astype(jnp.int32)
    slot = jnp.sum(hot * sub, axis=0, keepdims=True)
    partner = jnp.sum(hot * other_s, axis=0, keepdims=True)
    kept = jnp.sum(hot * keep, axis=0, keepdims=True)
    upto = jnp.sum((key_s <= lane).astype(jnp.int32), axis=0, keepdims=True)
    here = jnp.sum((key_s == lane).astype(jnp.int32), axis=0, keepdims=True)
    meta[base : base + 1, :] = slot
    meta[base + 1 : base + 2, :] = partner
    meta[base + 2 : base + 3, :] = kept
    meta[base + 3 : base + 4, :] = jnp.maximum(upto - 1, 0)
    meta[base + 4 : base + 5, :] = jnp.minimum(here, 1)


def kernel(
    n_row,
    n_col,
    scale,
    x_ref,
    w_hbm,
    b_hbm,
    tiles_hbm,
    trow_hbm,
    tcol_hbm,
    count_ref,
    ct_hbm,
    out_ref,
    gf_ref,
    gw_ref,
    gb_ref,
    w_ref,
    b_ref,
    trow_ref,
    tcol_ref,
    panel,
    tiles,
    ct,
    meta_v,
    meta,
    runs,
    rs_send,
    rs_recv,
    grads,
    sib_send,
    sib_recv,
    ring_send,
    ring_recv,
    wz_send,
    wz_recv,
    wc_send,
    wc_recv,
    wx_send,
    wx_recv,
    wg_send,
    wg_recv,
    local_sem,
    ag_ss,
    ag_rs,
    sib_ss,
    sib_rs,
    col_ss,
    col_rs,
    sr_ss,
    sr_rs,
    ring_ss,
    ring_rs,
    w_ss,
    w_rs,
):
    nz = n_row // 4
    ny = n_col // 2
    cap = tiles_hbm.shape[0]
    chunk = gw_ref.shape[0] // nz
    row = lax.axis_index("row")
    col = lax.axis_index("col")
    core = row % 2
    z = (row // 2) % nz
    xh = row // (2 * nz)
    y = col // 2
    xl = col % 2

    def rid(a, dz, other=0):
        xx = xh if a == 0 else 1 - xh
        kk = core if other == 0 else 1 - core
        return (xx * nz + (z + dz + nz) % nz) * 2 + kk

    def cid(dy, dx):
        return ((y + dy + ny) % ny) * 2 + (xl + dx) % 2

    def pair(index):
        return pl.ds(2 * index, 2)

    def send(src, dst, ss, rs, to_row=None, to_col=None):
        return pltpu.make_async_remote_copy(
            src_ref=src,
            dst_ref=dst,
            send_sem=ss,
            recv_sem=rs,
            device_id={
                "row": row if to_row is None else to_row,
                "col": col if to_col is None else to_col,
            },
            device_id_type=pl.DeviceIdType.MESH,
        )

    started = []

    def go(copy):
        copy.start()
        started.append(copy)

    sibling = rid(0, 0, 1)
    across = rid(1, 0)
    shifts = sorted(
        ((dy, dx) for dy in range(ny) for dx in range(2) if dy or dx),
        key=lambda p: -(min(p[0], ny - p[0]) + p[1]),
    )

    loads = [
        pltpu.make_async_copy(src, dst, local_sem.at[i])
        for i, (src, dst) in enumerate(
            (
                (trow_hbm, trow_ref),
                (tcol_hbm, tcol_ref),
                (x_ref, panel.at[pair(row)]),
                (w_hbm, w_ref),
                (b_hbm, b_ref),
                (ct_hbm, ct),
                (tiles_hbm, tiles),
            )
        )
    ]
    for load in loads:
        load.start()

    barrier = pltpu.get_barrier_semaphore()
    greet = [sibling, across] + [rid(0, d) for d in (1, 2, -1, -2)]
    for other in greet:
        pl.semaphore_signal(
            barrier, inc=1, device_id={"row": other, "col": col},
            device_id_type=pl.DeviceIdType.MESH,
        )
    for shift in shifts:
        pl.semaphore_signal(
            barrier, inc=1, device_id={"row": row, "col": cid(*shift)},
            device_id_type=pl.DeviceIdType.MESH,
        )
    pl.semaphore_wait(barrier, len(greet) + len(shifts))

    def ag(a, dz, t, to, src=None):
        k = (a * nz + dz % nz) * 2 + t
        if src is None:
            src = rid(a, dz)
        return send(
            x_ref.at[pl.ds(t, 1)] if to is not None and src is row else panel.at[pl.ds(2 * src + t, 1)],
            panel.at[pl.ds(2 * src + t, 1)],
            ag_ss.at[k],
            ag_rs.at[k],
            across if to is None else to,
        )

    def ag_wait(a, dz, t):
        ag(a, dz, t, None).wait_recv()

    def to_sibling(a, dz):
        k = a * nz + dz % nz
        blk = rid(a, dz)
        src = x_ref if a == 0 and dz == 0 else panel.at[pair(blk)]
        go(send(src, panel.at[pair(blk)], sib_ss.at[k], sib_rs.at[k], sibling))

    signs = (1, -1)
    for t in (0, 1):
        for e in signs:
            go(ag(0, -2 * e, t, rid(0, 2 * e), row))
        go(ag(1, 0, t, across, row))
    for t in (0, 1):
        for e in signs:
            go(ag(0, -e, t, rid(0, e), row))
    to_sibling(0, 0)

    for load in loads[:2]:
        load.wait()
    lane1 = lax.broadcasted_iota(jnp.int32, (1, SIDE), 1)
    live = lane1 < count_ref[0, 0]
    sort_plan(trow_ref[...], tcol_ref[...], live, meta_v, 0)
    sort_plan(tcol_ref[...], trow_ref[...], live, meta_v, 5)
    load_m = pltpu.make_async_copy(meta_v, meta, local_sem.at[7])
    load_m.start()

    for t in (0, 1):
        for e in signs:
            ag_wait(0, -2 * e, t)
            go(ag(1, -2 * e, t, across, rid(0, -2 * e)))
    for t in (0, 1):
        ag_wait(1, 0, t)
        for e in signs:
            go(ag(0, -3 * e, t, rid(0, e), rid(0, -2 * e)))
            go(ag(1, -e, t, rid(0, e), across))
    for t, e in enumerate(signs):
        go(ag(0, 4, t, rid(0, 2 * e), rid(0, -2 * e)))
    for e in signs:
        to_sibling(0, -2 * e)
    to_sibling(1, 0)
    for e in signs:
        for t in (0, 1):
            ag_wait(0, -e, t)
        to_sibling(0, -e)
    for t in (0, 1):
        for e in signs:
            ag_wait(1, -2 * e, t)
            if t == (0 if e == 1 else 1):
                go(ag(1, 4, t, rid(0, 2 * e), rid(1, -2 * e)))
            go(ag(1, -3 * e, t, rid(0, e), rid(1, -2 * e)))
    for e in signs:
        to_sibling(1, -2 * e)
    for a, dz in ((0, -3), (0, 3), (1, -1), (1, 1), (0, 4), (1, -3), (1, 3), (1, 4)):
        for t in (0, 1):
            ag_wait(a, dz, t)
        to_sibling(a, dz)
    for dz in (0, -2, 2, -1, 1, -3, 3, 4):
        for a in (0, 1):
            k = a * nz + dz % nz
            dst = panel.at[pair(rid(a, dz, 1))]
            send(dst, dst, sib_ss.at[k], sib_rs.at[k], sibling).wait_recv()
    for load in loads[2:]:
        load.wait()
    load_m.wait()

    def products(base, forward):
        def turn(i, acc):
            for u in range(UNROLL):
                s = i * UNROLL + u
                tile = tiles[meta[base, s]]
                if forward:
                    prod = jnp.dot(tile, panel[meta[base + 1, s]], preferred_element_type=F32)
                else:
                    prod = jnp.dot(grads[meta[base + 1, s]], tile, preferred_element_type=F32)
                acc = acc * meta[base + 2, s].astype(F32) + prod
                runs[s] = acc
            return acc

        lax.fori_loop(0, cap // UNROLL, turn, jnp.zeros((SIDE, SIDE), F32))

    def total(base, index):
        return runs[meta[base + 3, index]] * meta[base + 4, index].astype(F32)

    products(0, True)

    def cc(src, dst, k, to):
        return send(src, dst, col_ss.at[k], col_rs.at[k], None, to)

    for t in (0, 1):
        for j, shift in enumerate(shifts):
            i = 2 * cid(*shift) + t
            rs_send[i] = total(0, i).astype(BF16)
            mine = rs_recv.at[pl.ds(2 * col + t, 1)]
            go(cc(rs_send.at[pl.ds(i, 1)], mine, t * n_col + j, cid(*shift)))

    w = w_ref[...]
    agg = []
    gps = []
    outs = []
    for t in (0, 1):
        value = total(0, 2 * col + t)
        for j, (dy, dx) in reversed(list(enumerate(shifts))):
            src = cid(-dy, dx)
            i = 2 * src + t
            cc(rs_send.at[pl.ds(i, 1)], rs_recv.at[pl.ds(i, 1)], t * n_col + j, src).wait_recv()
            value = value + rs_recv[i].astype(F32)
        agg.append(value)
        hi = value.astype(BF16)
        lo = (value - hi.astype(F32)).astype(BF16)
        pre = jnp.dot(hi, w, preferred_element_type=F32) + jnp.dot(lo, w, preferred_element_type=F32)
        pre = pre + b_ref[...]
        sig = jax.nn.sigmoid(pre)
        outs.append((pre * sig).astype(BF16))
        slope = sig * (1.0 + pre * (1.0 - sig))
        gp = (ct[t * SIDE : (t + 1) * SIDE, :].astype(F32) * slope).astype(BF16)
        gps.append(gp)
        back = lax.dot_general(w, gp, (((1,), (1,)), ((), ())), preferred_element_type=F32)
        grads[2 * col + t] = back.astype(BF16)
        own = grads.at[pl.ds(2 * col + t, 1)]
        for j, shift in enumerate(shifts):
            go(cc(own, own, (2 + t) * n_col + j, cid(*shift)))

    bias = jnp.sum(gps[0].astype(F32), axis=0, keepdims=True) + jnp.sum(gps[1].astype(F32), axis=0, keepdims=True)
    dw = jnp.zeros(gw_ref.shape, F32)
    for t in (0, 1):
        turned = agg[t].T
        hi = turned.astype(BF16)
        lo = (turned - hi.astype(F32)).astype(BF16)
        dw = dw + jnp.dot(hi, gps[t], preferred_element_type=F32)
        dw = dw + jnp.dot(lo, gps[t], preferred_element_type=F32)
    bias8 = jnp.broadcast_to(bias, (8, bias.shape[1]))
    for c in range(nz):
        wz_send[c, :chunk, :] = dw[c * chunk : (c + 1) * chunk, :]
        wz_send[c, chunk:, :] = bias8
    wz_recv[z] = wz_send[z]

    def wcopy(src, dst, k, to_row=None, to_col=None):
        return send(src, dst, w_ss.at[k], w_rs.at[k], to_row, to_col)

    far = sorted(range(1, nz), key=lambda d: -min(d, nz - d))
    for d in far:
        go(wcopy(wz_send.at[(z + d) % nz], wz_recv.at[z], d, rid(0, d)))
    for t in (0, 1):
        out_ref[t * SIDE : (t + 1) * SIDE, :] = outs[t]

    for t in (0, 1):
        for j, (dy, dx) in enumerate(shifts):
            src = cid(-dy, dx)
            there = grads.at[pl.ds(2 * src + t, 1)]
            cc(there, there, (2 + t) * n_col + j, src).wait_recv()

    products(5, False)

    def added(ref, n):
        value = ref[0]
        for i in range(1, n):
            value = value + ref[i]
        return value

    def over_z_done():
        for d in far:
            src = (z - d + nz) % nz
            wcopy(wz_send.at[src], wz_recv.at[src], d, rid(0, -d)).wait_recv()
        value = added(wz_recv, nz)
        wc_send[...] = value
        wc_recv[col] = value
        for j, shift in enumerate(shifts):
            go(wcopy(wc_send, wc_recv.at[col], nz + j, None, cid(*shift)))

    quad = 2 * xh + core
    quads = ((1, 1), (1, 0), (0, 1))

    def over_col_done():
        for j, (dy, dx) in enumerate(shifts):
            src = cid(-dy, dx)
            wcopy(wc_send, wc_recv.at[src], nz + j, None, src).wait_recv()
        value = added(wc_recv, n_col)
        wx_send[...] = value
        wx_recv[quad] = value
        for j, (a, other) in enumerate(quads):
            go(wcopy(wx_send, wx_recv.at[quad], nz + n_col + j, rid(a, 0, other)))

    def over_quad_done():
        for j, (a, other) in enumerate(quads):
            src = 2 * (xh if a == 0 else 1 - xh) + (core if other == 0 else 1 - core)
            wcopy(wx_send, wx_recv.at[src], nz + n_col + j, rid(a, 0, other)).wait_recv()
        value = added(wx_recv, 4) * scale
        gb_ref[...] = value[chunk : chunk + 1, :]
        wg_send[...] = value[:chunk, :]
        wg_recv[z] = value[:chunk, :]
        for d in far:
            go(wcopy(wg_send, wg_recv.at[z], nz + n_col + 4 + d, rid(0, d)))

    def gathered():
        for d in far:
            src = (z - d + nz) % nz
            wcopy(wg_send, wg_recv.at[src], nz + n_col + 4 + d, rid(0, -d)).wait_recv()
        for c in range(nz):
            gw_ref[c * chunk : (c + 1) * chunk, :] = wg_recv[c]

    order = [(1, 3), (1, -3), (1, 4), (0, 3), (0, -3), (0, 4), (1, 2), (1, -2)]
    order += [(1, 1), (1, -1), (0, 1), (0, -1), (0, 2), (0, -2), (1, 0), (0, 0)]

    def sib_copy(a, dz):
        k = a * nz + dz % nz
        return send(sib_send.at[k], sib_recv.at[k], sr_ss.at[k], sr_rs.at[k], sibling)

    for a, dz in order:
        for t in (0, 1):
            sib_send[a * nz + dz % nz, t] = total(5, 2 * rid(a, dz, 1) + t).astype(BF16)
        go(sib_copy(a, dz))
    over_z_done()

    def comb(a, dz, t):
        return total(5, 2 * rid(a, dz) + t) + sib_recv[a * nz + dz % nz, t].astype(F32)

    slots = {}
    for a in (0, 1):
        for e in signs:
            for name in ("three", "four", "one"):
                slots[name, a, e] = len(slots)
    for e in signs:
        slots["cross", 0, e] = len(slots)
        slots["two", 0, e] = len(slots)
    slots["zero", 0, 1] = len(slots)

    def ring(name, a, e, t, to):
        k = slots[name, a, e]
        return send(
            ring_send.at[k, pl.ds(t, 1)],
            ring_recv.at[k, pl.ds(t, 1)],
            ring_ss.at[2 * k + t],
            ring_rs.at[2 * k + t],
            to,
        )

    def ring_go(name, a, e, t, to, value):
        ring_send[slots[name, a, e], t] = value.astype(BF16)
        go(ring(name, a, e, t, to))

    def arrived(name, a, e, t):
        ring(name, a, e, t, across).wait_recv()
        return ring_recv[slots[name, a, e], t].astype(F32)

    for a in (1, 0):
        for e in signs:
            sib_copy(a, 3 * e).wait_recv()
            for t in (0, 1):
                ring_go("three", a, e, t, rid(0, e), comb(a, 3 * e, t))
        sib_copy(a, 4).wait_recv()
        for t, e in enumerate((-1, 1)):
            ring_go("four", a, e, t, rid(0, 2 * e), comb(a, 4, t))
    for a in (1, 0):
        for e in signs:
            sib_copy(a, e).wait_recv()
            for t in (0, 1):
                ring_go("one", a, e, t, rid(0, e), comb(a, e, t))

    def near(a, e, t):
        value = comb(a, 2 * e, t) + arrived("three", a, e, t)
        if t == (0 if e == -1 else 1):
            value = value + arrived("four", a, e, t)
        return value

    for e in signs:
        sib_copy(1, 2 * e).wait_recv()
    for t in (0, 1):
        for e in signs:
            ring_go("cross", 0, e, t, across, near(1, e, t))
    over_col_done()
    sib_copy(1, 0).wait_recv()
    for t in (0, 1):
        value = comb(1, 0, t) + arrived("one", 1, 1, t) + arrived("one", 1, -1, t)
        ring_go("zero", 0, 1, t, across, value)
    for e in signs:
        sib_copy(0, 2 * e).wait_recv()
    for t in (0, 1):
        for e in signs:
            value = near(0, e, t) + arrived("cross", 0, e, t)
            ring_go("two", 0, e, t, rid(0, 2 * e), value)
    over_quad_done()
    sib_copy(0, 0).wait_recv()
    for t in (0, 1):
        value = comb(0, 0, t)
        for e in signs:
            value = value + arrived("one", 0, e, t)
        value = value + arrived("zero", 0, 1, t)
        for e in signs:
            value = value + arrived("two", 0, e, t)
        gf_ref[t * SIDE : (t + 1) * SIDE, :] = value.T.astype(BF16)
    gathered()
    for copy in started:
        copy.wait_send()


def write_out(*refs):
    copies = [pltpu.make_async_copy(refs[i], refs[4 + i], refs[8].at[i]) for i in range(4)]
    for copy in copies:
        copy.start()
    for copy in copies:
        copy.wait()


def local(n_row, n_col, features, weight, bias, tile_values, tile_row, tile_col, tile_count, cotangent):
    nodes, f = features.shape
    h = weight.shape[1]
    cap = tile_values.shape[2]
    nz = n_row // 4
    chunk = f // nz
    scale = (n_row * n_col * nodes) ** (-0.5)
    pad = SIDE - tile_row.shape[-1]
    trow = jnp.pad(tile_row.reshape(1, -1), ((0, 0), (0, pad)))
    tcol = jnp.pad(tile_col.reshape(1, -1), ((0, 0), (0, pad)))
    vmem = pl.BlockSpec(memory_space=pltpu.VMEM)
    hbm = pl.BlockSpec(memory_space=pltpu.HBM)
    dma = pltpu.SemaphoreType.DMA
    square = (SIDE, SIDE)
    output, gf, gw, gb = pl.pallas_call(
        functools.partial(kernel, n_row, n_col, scale),
        out_shape=(
            jax.ShapeDtypeStruct((nodes, h), BF16),
            jax.ShapeDtypeStruct((nodes, f), BF16),
            jax.ShapeDtypeStruct((f, h), F32),
            jax.ShapeDtypeStruct((1, h), F32),
        ),
        in_specs=[hbm] * 6 + [pl.BlockSpec(memory_space=pltpu.SMEM), hbm],
        out_specs=(vmem,) * 4,
        scratch_shapes=[
            pltpu.VMEM((f, h), BF16),
            pltpu.VMEM((1, h), F32),
            pltpu.VMEM((1, SIDE), jnp.int32),
            pltpu.VMEM((1, SIDE), jnp.int32),
            pltpu.VMEM((2 * n_row,) + square, BF16),
            pltpu.VMEM((cap,) + square, BF16),
            pltpu.VMEM((nodes, h), BF16),
            pltpu.VMEM((16, SIDE), jnp.int32),
            pltpu.SMEM((16, SIDE), jnp.int32),
            pltpu.VMEM((cap,) + square, F32),
            pltpu.VMEM((2 * n_col,) + square, BF16),
            pltpu.VMEM((2 * n_col,) + square, BF16),
            pltpu.VMEM((2 * n_col,) + square, BF16),
            pltpu.VMEM((2 * nz, 2) + square, BF16),
            pltpu.VMEM((2 * nz, 2) + square, BF16),
            pltpu.VMEM((17, 2) + square, BF16),
            pltpu.VMEM((17, 2) + square, BF16),
            pltpu.VMEM((nz, chunk + 8, h), F32),
            pltpu.VMEM((nz, chunk + 8, h), F32),
            pltpu.VMEM((chunk + 8, h), F32),
            pltpu.VMEM((n_col, chunk + 8, h), F32),
            pltpu.VMEM((chunk + 8, h), F32),
            pltpu.VMEM((4, chunk + 8, h), F32),
            pltpu.VMEM((chunk, h), F32),
            pltpu.VMEM((nz, chunk, h), F32),
            dma((8,)),
            dma((4 * nz,)),
            dma((4 * nz,)),
            dma((2 * nz,)),
            dma((2 * nz,)),
            dma((4 * n_col,)),
            dma((4 * n_col,)),
            dma((2 * nz,)),
            dma((2 * nz,)),
            dma((34,)),
            dma((34,)),
            dma((2 * nz + n_col + 4,)),
            dma((2 * nz + n_col + 4,)),
        ],
        compiler_params=pltpu.CompilerParams(
            collective_id=0, has_side_effects=True, vmem_limit_bytes=48 * 1024 * 1024
        ),
    )(
        *(
            pltpu.with_memory_space_constraint(operand, pltpu.HBM)
            for operand in (
                features.reshape(2, SIDE, f),
                weight,
                bias.reshape(1, h),
                tile_values.reshape(tile_values.shape[2:]),
                trow,
                tcol,
            )
        ),
        tile_count,
        pltpu.with_memory_space_constraint(cotangent, pltpu.HBM),
    )
    results = (output, gf, gw, gb)
    output, gf, gw, gb = pl.pallas_call(
        write_out,
        out_shape=tuple(jax.ShapeDtypeStruct(a.shape, a.dtype) for a in results),
        in_specs=[pl.BlockSpec(memory_space=pl.ANY)] * 4,
        out_specs=(hbm,) * 4,
        scratch_shapes=[dma((4,))],
        compiler_params=pltpu.CompilerParams(vmem_limit_bytes=1024 * 1024),
    )(*(pltpu.with_memory_space_constraint(a, pltpu.VMEM) for a in results))
    return output, gf, gw, gb.reshape(h)


def solution(mesh):
    placed = (
        P(("col", "row"), None),
        P(),
        P(),
        P("row", "col", None, None, None),
        P("row", "col", None),
        P("row", "col", None),
        P("row", "col"),
        P(("row", "col"), None),
    )
    return jax.shard_map(
        functools.partial(local, mesh.shape["row"], mesh.shape["col"]),
        mesh=mesh,
        in_specs=placed,
        out_specs=(P(("row", "col"), None), P(("col", "row"), None), P(), P()),
        check_vma=False,
    )
```

```python
import functools

import jax
import jax.numpy as jnp
from jax import lax
from jax.experimental import pallas as pl
from jax.experimental.pallas import tpu as pltpu
from jax.sharding import PartitionSpec as P

F32 = jnp.float32
BF16 = jnp.bfloat16
SIDE = 128
UNROLL = 64


def sort_plan(key, other, live, meta, base):
    shape = (SIDE, SIDE)
    lane = lax.broadcasted_iota(jnp.int32, shape, 1)
    sub = lax.broadcasted_iota(jnp.int32, shape, 0)
    key_l = jnp.broadcast_to(jnp.where(live, key, SIDE), shape)
    key_s = key_l.T
    other_s = jnp.broadcast_to(other, shape).T
    less = (key_l < key_s) | ((key_l == key_s) & (lane < sub))
    rank = jnp.sum(less.astype(jnp.int32), axis=1, keepdims=True)
    same = (key_l == key_s) & (lane < sub)
    keep = jnp.minimum(jnp.sum(same.astype(jnp.int32), axis=1, keepdims=True), 1)
    hot = (rank == lane).astype(jnp.int32)
    slot = jnp.sum(hot * sub, axis=0, keepdims=True)
    partner = jnp.sum(hot * other_s, axis=0, keepdims=True)
    kept = jnp.sum(hot * keep, axis=0, keepdims=True)
    upto = jnp.sum((key_s <= lane).astype(jnp.int32), axis=0, keepdims=True)
    here = jnp.sum((key_s == lane).astype(jnp.int32), axis=0, keepdims=True)
    meta[base : base + 1, :] = slot
    meta[base + 1 : base + 2, :] = partner
    meta[base + 2 : base + 3, :] = kept
    meta[base + 3 : base + 4, :] = jnp.maximum(upto - 1, 0)
    meta[base + 4 : base + 5, :] = jnp.minimum(here, 1)


def kernel(
    n_row,
    n_col,
    scale,
    x_ref,
    w_hbm,
    b_hbm,
    tiles_hbm,
    trow_hbm,
    tcol_hbm,
    count_ref,
    ct_hbm,
    out_ref,
    gf_ref,
    gw_ref,
    gb_ref,
    w_ref,
    b_ref,
    trow_ref,
    tcol_ref,
    panel,
    tiles,
    ct,
    meta_v,
    meta,
    runs,
    rs_send,
    rs_recv,
    grads,
    sib_send,
    sib_recv,
    ring_send,
    ring_recv,
    wz_send,
    wz_recv,
    wc_send,
    wc_recv,
    wx_send,
    wx_recv,
    wg_send,
    wg_recv,
    local_sem,
    ag_ss,
    ag_rs,
    sib_ss,
    sib_rs,
    col_ss,
    col_rs,
    sr_ss,
    sr_rs,
    ring_ss,
    ring_rs,
    w_ss,
    w_rs,
):
    nz = n_row // 4
    ny = n_col // 2
    cap = tiles_hbm.shape[0]
    chunk = gw_ref.shape[0] // nz
    row = lax.axis_index("row")
    col = lax.axis_index("col")
    core = row % 2
    z = (row // 2) % nz
    xh = row // (2 * nz)
    y = col // 2
    xl = col % 2

    def rid(a, dz, other=0):
        xx = xh if a == 0 else 1 - xh
        kk = core if other == 0 else 1 - core
        return (xx * nz + (z + dz + nz) % nz) * 2 + kk

    def cid(dy, dx):
        return ((y + dy + ny) % ny) * 2 + (xl + dx) % 2

    def pair(index):
        return pl.ds(2 * index, 2)

    def send(src, dst, ss, rs, to_row=None, to_col=None):
        return pltpu.make_async_remote_copy(
            src_ref=src,
            dst_ref=dst,
            send_sem=ss,
            recv_sem=rs,
            device_id={
                "row": row if to_row is None else to_row,
                "col": col if to_col is None else to_col,
            },
            device_id_type=pl.DeviceIdType.MESH,
        )

    started = []

    def go(copy):
        copy.start()
        started.append(copy)

    def drain(keep):
        for copy in started[: len(started) - keep]:
            copy.wait_send()
        del started[: len(started) - keep]

    sibling = rid(0, 0, 1)
    across = rid(1, 0)
    shifts = sorted(
        ((dy, dx) for dy in range(ny) for dx in range(2) if dy or dx),
        key=lambda p: -(min(p[0], ny - p[0]) + p[1]),
    )

    loads = [
        pltpu.make_async_copy(src, dst, local_sem.at[i])
        for i, (src, dst) in enumerate(
            (
                (trow_hbm, trow_ref),
                (tcol_hbm, tcol_ref),
                (x_ref, panel.at[pair(row)]),
                (w_hbm, w_ref),
                (b_hbm, b_ref),
                (ct_hbm, ct),
                (tiles_hbm, tiles),
            )
        )
    ]
    for load in loads:
        load.start()

    barrier = pltpu.get_barrier_semaphore()
    greet = [sibling, across] + [rid(0, d) for d in (1, 2, -1, -2)]
    for other in greet:
        pl.semaphore_signal(
            barrier, inc=1, device_id={"row": other, "col": col},
            device_id_type=pl.DeviceIdType.MESH,
        )
    for shift in shifts:
        pl.semaphore_signal(
            barrier, inc=1, device_id={"row": row, "col": cid(*shift)},
            device_id_type=pl.DeviceIdType.MESH,
        )
    pl.semaphore_wait(barrier, len(greet) + len(shifts))

    def ag(a, dz, t, to, src=None):
        k = (a * nz + dz % nz) * 2 + t
        if src is None:
            src = rid(a, dz)
        return send(
            x_ref.at[pl.ds(t, 1)] if to is not None and src is row else panel.at[pl.ds(2 * src + t, 1)],
            panel.at[pl.ds(2 * src + t, 1)],
            ag_ss.at[k],
            ag_rs.at[k],
            across if to is None else to,
        )

    def ag_wait(a, dz, t):
        ag(a, dz, t, None).wait_recv()

    def to_sibling(a, dz):
        k = a * nz + dz % nz
        blk = rid(a, dz)
        src = x_ref if a == 0 and dz == 0 else panel.at[pair(blk)]
        go(send(src, panel.at[pair(blk)], sib_ss.at[k], sib_rs.at[k], sibling))

    signs = (1, -1)
    for t in (0, 1):
        for e in signs:
            go(ag(0, -2 * e, t, rid(0, 2 * e), row))
        go(ag(1, 0, t, across, row))
    for t in (0, 1):
        for e in signs:
            go(ag(0, -e, t, rid(0, e), row))
    to_sibling(0, 0)

    for load in loads[:2]:
        load.wait()
    lane1 = lax.broadcasted_iota(jnp.int32, (1, SIDE), 1)
    live = lane1 < count_ref[0, 0]
    sort_plan(trow_ref[...], tcol_ref[...], live, meta_v, 0)
    sort_plan(tcol_ref[...], trow_ref[...], live, meta_v, 5)
    load_m = pltpu.make_async_copy(meta_v, meta, local_sem.at[7])
    load_m.start()

    for t in (0, 1):
        for e in signs:
            ag_wait(0, -2 * e, t)
            go(ag(1, -2 * e, t, across, rid(0, -2 * e)))
    for t in (0, 1):
        ag_wait(1, 0, t)
        for e in signs:
            go(ag(0, -3 * e, t, rid(0, e), rid(0, -2 * e)))
            go(ag(1, -e, t, rid(0, e), across))
    for t, e in enumerate(signs):
        go(ag(0, 4, t, rid(0, 2 * e), rid(0, -2 * e)))
    for e in signs:
        to_sibling(0, -2 * e)
    to_sibling(1, 0)
    for e in signs:
        for t in (0, 1):
            ag_wait(0, -e, t)
        to_sibling(0, -e)
    for t in (0, 1):
        for e in signs:
            ag_wait(1, -2 * e, t)
            if t == (0 if e == 1 else 1):
                go(ag(1, 4, t, rid(0, 2 * e), rid(1, -2 * e)))
            go(ag(1, -3 * e, t, rid(0, e), rid(1, -2 * e)))
    for e in signs:
        to_sibling(1, -2 * e)
    for a, dz in ((0, -3), (0, 3), (1, -1), (1, 1), (0, 4), (1, -3), (1, 3), (1, 4)):
        for t in (0, 1):
            ag_wait(a, dz, t)
        to_sibling(a, dz)
    for dz in (0, -2, 2, -1, 1, -3, 3, 4):
        for a in (0, 1):
            k = a * nz + dz % nz
            dst = panel.at[pair(rid(a, dz, 1))]
            send(dst, dst, sib_ss.at[k], sib_rs.at[k], sibling).wait_recv()
    for load in loads[2:]:
        load.wait()
    load_m.wait()

    def products(base, forward):
        def turn(i, acc):
            for u in range(UNROLL):
                s = i * UNROLL + u
                tile = tiles[meta[base, s]]
                if forward:
                    prod = jnp.dot(tile, panel[meta[base + 1, s]], preferred_element_type=F32)
                else:
                    prod = jnp.dot(grads[meta[base + 1, s]], tile, preferred_element_type=F32)
                acc = acc * meta[base + 2, s].astype(F32) + prod
                runs[s] = acc
            return acc

        lax.fori_loop(0, cap // UNROLL, turn, jnp.zeros((SIDE, SIDE), F32))

    def total(base, index):
        return runs[meta[base + 3, index]] * meta[base + 4, index].astype(F32)

    products(0, True)

    def cc(src, dst, k, to):
        return send(src, dst, col_ss.at[k], col_rs.at[k], None, to)

    for t in (0, 1):
        for j, shift in enumerate(shifts):
            i = 2 * cid(*shift) + t
            rs_send[i] = total(0, i).astype(BF16)
            mine = rs_recv.at[pl.ds(2 * col + t, 1)]
            go(cc(rs_send.at[pl.ds(i, 1)], mine, t * n_col + j, cid(*shift)))

    drain(2 * len(shifts))
    w = w_ref[...]
    agg = []
    gps = []
    outs = []
    for t in (0, 1):
        value = total(0, 2 * col + t)
        for j, (dy, dx) in reversed(list(enumerate(shifts))):
            src = cid(-dy, dx)
            i = 2 * src + t
            cc(rs_send.at[pl.ds(i, 1)], rs_recv.at[pl.ds(i, 1)], t * n_col + j, src).wait_recv()
            value = value + rs_recv[i].astype(F32)
        agg.append(value)
        hi = value.astype(BF16)
        lo = (value - hi.astype(F32)).astype(BF16)
        pre = jnp.dot(hi, w, preferred_element_type=F32) + jnp.dot(lo, w, preferred_element_type=F32)
        pre = pre + b_ref[...]
        sig = jax.nn.sigmoid(pre)
        outs.append((pre * sig).astype(BF16))
        slope = sig * (1.0 + pre * (1.0 - sig))
        gp = (ct[t * SIDE : (t + 1) * SIDE, :].astype(F32) * slope).astype(BF16)
        gps.append(gp)
        back = lax.dot_general(w, gp, (((1,), (1,)), ((), ())), preferred_element_type=F32)
        grads[2 * col + t] = back.astype(BF16)
        own = grads.at[pl.ds(2 * col + t, 1)]
        for j, shift in enumerate(shifts):
            go(cc(own, own, (2 + t) * n_col + j, cid(*shift)))

    bias = jnp.sum(gps[0].astype(F32), axis=0, keepdims=True) + jnp.sum(gps[1].astype(F32), axis=0, keepdims=True)
    dw = jnp.zeros(gw_ref.shape, F32)
    for t in (0, 1):
        turned = agg[t].T
        hi = turned.astype(BF16)
        lo = (turned - hi.astype(F32)).astype(BF16)
        dw = dw + jnp.dot(hi, gps[t], preferred_element_type=F32)
        dw = dw + jnp.dot(lo, gps[t], preferred_element_type=F32)
    bias8 = jnp.broadcast_to(bias, (8, bias.shape[1]))
    for c in range(nz):
        wz_send[c, :chunk, :] = dw[c * chunk : (c + 1) * chunk, :]
        wz_send[c, chunk:, :] = bias8
    wz_recv[z] = wz_send[z]

    def wcopy(src, dst, k, to_row=None, to_col=None):
        return send(src, dst, w_ss.at[k], w_rs.at[k], to_row, to_col)

    far = sorted(range(1, nz), key=lambda d: -min(d, nz - d))
    for d in far:
        go(wcopy(wz_send.at[(z + d) % nz], wz_recv.at[z], d, rid(0, d)))
    for t in (0, 1):
        out_ref[t * SIDE : (t + 1) * SIDE, :] = outs[t]

    drain(2 * len(shifts) + len(far))
    for t in (0, 1):
        for j, (dy, dx) in enumerate(shifts):
            src = cid(-dy, dx)
            there = grads.at[pl.ds(2 * src + t, 1)]
            cc(there, there, (2 + t) * n_col + j, src).wait_recv()

    products(5, False)

    def added(ref, n):
        value = ref[0]
        for i in range(1, n):
            value = value + ref[i]
        return value

    def over_z_done():
        for d in far:
            src = (z - d + nz) % nz
            wcopy(wz_send.at[src], wz_recv.at[src], d, rid(0, -d)).wait_recv()
        value = added(wz_recv, nz)
        wc_send[...] = value
        wc_recv[col] = value
        for j, shift in enumerate(shifts):
            go(wcopy(wc_send, wc_recv.at[col], nz + j, None, cid(*shift)))

    quad = 2 * xh + core
    quads = ((1, 1), (1, 0), (0, 1))

    def over_col_done():
        for j, (dy, dx) in enumerate(shifts):
            src = cid(-dy, dx)
            wcopy(wc_send, wc_recv.at[src], nz + j, None, src).wait_recv()
        value = added(wc_recv, n_col)
        wx_send[...] = value
        wx_recv[quad] = value
        for j, (a, other) in enumerate(quads):
            go(wcopy(wx_send, wx_recv.at[quad], nz + n_col + j, rid(a, 0, other)))

    def over_quad_done():
        for j, (a, other) in enumerate(quads):
            src = 2 * (xh if a == 0 else 1 - xh) + (core if other == 0 else 1 - core)
            wcopy(wx_send, wx_recv.at[src], nz + n_col + j, rid(a, 0, other)).wait_recv()
        value = added(wx_recv, 4) * scale
        gb_ref[...] = value[chunk : chunk + 1, :]
        wg_send[...] = value[:chunk, :]
        wg_recv[z] = value[:chunk, :]
        for d in far:
            go(wcopy(wg_send, wg_recv.at[z], nz + n_col + 4 + d, rid(0, d)))

    def gathered():
        for d in far:
            src = (z - d + nz) % nz
            wcopy(wg_send, wg_recv.at[src], nz + n_col + 4 + d, rid(0, -d)).wait_recv()
        for c in range(nz):
            gw_ref[c * chunk : (c + 1) * chunk, :] = wg_recv[c]

    order = [(1, 3), (1, -3), (1, 4), (0, 3), (0, -3), (0, 4), (1, 2), (1, -2)]
    order += [(1, 1), (1, -1), (0, 1), (0, -1), (0, 2), (0, -2), (1, 0), (0, 0)]

    def sib_copy(a, dz):
        k = a * nz + dz % nz
        return send(sib_send.at[k], sib_recv.at[k], sr_ss.at[k], sr_rs.at[k], sibling)

    for a, dz in order:
        for t in (0, 1):
            sib_send[a * nz + dz % nz, t] = total(5, 2 * rid(a, dz, 1) + t).astype(BF16)
        go(sib_copy(a, dz))
    over_z_done()

    def comb(a, dz, t):
        return total(5, 2 * rid(a, dz) + t) + sib_recv[a * nz + dz % nz, t].astype(F32)

    slots = {}
    for a in (0, 1):
        for e in signs:
            for name in ("three", "four", "one"):
                slots[name, a, e] = len(slots)
    for e in signs:
        slots["cross", 0, e] = len(slots)
        slots["two", 0, e] = len(slots)
    slots["zero", 0, 1] = len(slots)

    def ring(name, a, e, t, to):
        k = slots[name, a, e]
        return send(
            ring_send.at[k, pl.ds(t, 1)],
            ring_recv.at[k, pl.ds(t, 1)],
            ring_ss.at[2 * k + t],
            ring_rs.at[2 * k + t],
            to,
        )

    def ring_go(name, a, e, t, to, value):
        ring_send[slots[name, a, e], t] = value.astype(BF16)
        go(ring(name, a, e, t, to))

    def arrived(name, a, e, t):
        ring(name, a, e, t, across).wait_recv()
        return ring_recv[slots[name, a, e], t].astype(F32)

    for a in (1, 0):
        for e in signs:
            sib_copy(a, 3 * e).wait_recv()
            for t in (0, 1):
                ring_go("three", a, e, t, rid(0, e), comb(a, 3 * e, t))
        sib_copy(a, 4).wait_recv()
        for t, e in enumerate((-1, 1)):
            ring_go("four", a, e, t, rid(0, 2 * e), comb(a, 4, t))
    for a in (1, 0):
        for e in signs:
            sib_copy(a, e).wait_recv()
            for t in (0, 1):
                ring_go("one", a, e, t, rid(0, e), comb(a, e, t))

    drain(24)

    def near(a, e, t):
        value = comb(a, 2 * e, t) + arrived("three", a, e, t)
        if t == (0 if e == -1 else 1):
            value = value + arrived("four", a, e, t)
        return value

    for e in signs:
        sib_copy(1, 2 * e).wait_recv()
    for t in (0, 1):
        for e in signs:
            ring_go("cross", 0, e, t, across, near(1, e, t))
    over_col_done()
    sib_copy(1, 0).wait_recv()
    for t in (0, 1):
        value = comb(1, 0, t) + arrived("one", 1, 1, t) + arrived("one", 1, -1, t)
        ring_go("zero", 0, 1, t, across, value)
    for e in signs:
        sib_copy(0, 2 * e).wait_recv()
    for t in (0, 1):
        for e in signs:
            value = near(0, e, t) + arrived("cross", 0, e, t)
            ring_go("two", 0, e, t, rid(0, 2 * e), value)
    over_quad_done()
    drain(2 * len(signs) + len(far))
    sib_copy(0, 0).wait_recv()
    for t in (0, 1):
        value = comb(0, 0, t)
        for e in signs:
            value = value + arrived("one", 0, e, t)
        value = value + arrived("zero", 0, 1, t)
        for e in signs:
            value = value + arrived("two", 0, e, t)
        gf_ref[t * SIDE : (t + 1) * SIDE, :] = value.T.astype(BF16)
    gathered()
    drain(0)


def write_out(*refs):
    copies = [pltpu.make_async_copy(refs[i], refs[4 + i], refs[8].at[i]) for i in range(4)]
    for copy in copies:
        copy.start()
    for copy in copies:
        copy.wait()


def local(n_row, n_col, features, weight, bias, tile_values, tile_row, tile_col, tile_count, cotangent):
    nodes, f = features.shape
    h = weight.shape[1]
    cap = tile_values.shape[2]
    nz = n_row // 4
    chunk = f // nz
    scale = (n_row * n_col * nodes) ** (-0.5)
    pad = SIDE - tile_row.shape[-1]
    trow = jnp.pad(tile_row.reshape(1, -1), ((0, 0), (0, pad)))
    tcol = jnp.pad(tile_col.reshape(1, -1), ((0, 0), (0, pad)))
    vmem = pl.BlockSpec(memory_space=pltpu.VMEM)
    hbm = pl.BlockSpec(memory_space=pltpu.HBM)
    dma = pltpu.SemaphoreType.DMA
    square = (SIDE, SIDE)
    output, gf, gw, gb = pl.pallas_call(
        functools.partial(kernel, n_row, n_col, scale),
        out_shape=(
            jax.ShapeDtypeStruct((nodes, h), BF16),
            jax.ShapeDtypeStruct((nodes, f), BF16),
            jax.ShapeDtypeStruct((f, h), F32),
            jax.ShapeDtypeStruct((1, h), F32),
        ),
        in_specs=[hbm] * 6 + [pl.BlockSpec(memory_space=pltpu.SMEM), hbm],
        out_specs=(vmem,) * 4,
        scratch_shapes=[
            pltpu.VMEM((f, h), BF16),
            pltpu.VMEM((1, h), F32),
            pltpu.VMEM((1, SIDE), jnp.int32),
            pltpu.VMEM((1, SIDE), jnp.int32),
            pltpu.VMEM((2 * n_row,) + square, BF16),
            pltpu.VMEM((cap,) + square, BF16),
            pltpu.VMEM((nodes, h), BF16),
            pltpu.VMEM((16, SIDE), jnp.int32),
            pltpu.SMEM((16, SIDE), jnp.int32),
            pltpu.VMEM((cap,) + square, F32),
            pltpu.VMEM((2 * n_col,) + square, BF16),
            pltpu.VMEM((2 * n_col,) + square, BF16),
            pltpu.VMEM((2 * n_col,) + square, BF16),
            pltpu.VMEM((2 * nz, 2) + square, BF16),
            pltpu.VMEM((2 * nz, 2) + square, BF16),
            pltpu.VMEM((17, 2) + square, BF16),
            pltpu.VMEM((17, 2) + square, BF16),
            pltpu.VMEM((nz, chunk + 8, h), F32),
            pltpu.VMEM((nz, chunk + 8, h), F32),
            pltpu.VMEM((chunk + 8, h), F32),
            pltpu.VMEM((n_col, chunk + 8, h), F32),
            pltpu.VMEM((chunk + 8, h), F32),
            pltpu.VMEM((4, chunk + 8, h), F32),
            pltpu.VMEM((chunk, h), F32),
            pltpu.VMEM((nz, chunk, h), F32),
            dma((8,)),
            dma((4 * nz,)),
            dma((4 * nz,)),
            dma((2 * nz,)),
            dma((2 * nz,)),
            dma((4 * n_col,)),
            dma((4 * n_col,)),
            dma((2 * nz,)),
            dma((2 * nz,)),
            dma((34,)),
            dma((34,)),
            dma((2 * nz + n_col + 4,)),
            dma((2 * nz + n_col + 4,)),
        ],
        compiler_params=pltpu.CompilerParams(
            collective_id=0, has_side_effects=True, vmem_limit_bytes=48 * 1024 * 1024
        ),
    )(
        *(
            pltpu.with_memory_space_constraint(operand, pltpu.HBM)
            for operand in (
                features.reshape(2, SIDE, f),
                weight,
                bias.reshape(1, h),
                tile_values.reshape(tile_values.shape[2:]),
                trow,
                tcol,
            )
        ),
        tile_count,
        pltpu.with_memory_space_constraint(cotangent, pltpu.HBM),
    )
    results = (output, gf, gw, gb)
    output, gf, gw, gb = pl.pallas_call(
        write_out,
        out_shape=tuple(jax.ShapeDtypeStruct(a.shape, a.dtype) for a in results),
        in_specs=[pl.BlockSpec(memory_space=pl.ANY)] * 4,
        out_specs=(hbm,) * 4,
        scratch_shapes=[dma((4,))],
        compiler_params=pltpu.CompilerParams(vmem_limit_bytes=1024 * 1024),
    )(*(pltpu.with_memory_space_constraint(a, pltpu.VMEM) for a in results))
    return output, gf, gw, gb.reshape(h)


def solution(mesh):
    placed = (
        P(("col", "row"), None),
        P(),
        P(),
        P("row", "col", None, None, None),
        P("row", "col", None),
        P("row", "col", None),
        P("row", "col"),
        P(("row", "col"), None),
    )
    return jax.shard_map(
        functools.partial(local, mesh.shape["row"], mesh.shape["col"]),
        mesh=mesh,
        in_specs=placed,
        out_specs=(P(("row", "col"), None), P(("col", "row"), None), P(), P()),
        check_vma=False,
    )
```

```python
import functools

import jax
import jax.numpy as jnp
from jax import lax
from jax.experimental import pallas as pl
from jax.experimental.pallas import tpu as pltpu
from jax.sharding import PartitionSpec as P

F32 = jnp.float32
BF16 = jnp.bfloat16
SIDE = 128
UNROLL = 64


def sort_plan(key, other, live, meta, base):
    shape = (SIDE, SIDE)
    lane = lax.broadcasted_iota(jnp.int32, shape, 1)
    sub = lax.broadcasted_iota(jnp.int32, shape, 0)
    key_l = jnp.broadcast_to(jnp.where(live, key, SIDE), shape)
    key_s = key_l.T
    other_s = jnp.broadcast_to(other, shape).T
    less = (key_l < key_s) | ((key_l == key_s) & (lane < sub))
    rank = jnp.sum(less.astype(jnp.int32), axis=1, keepdims=True)
    same = (key_l == key_s) & (lane < sub)
    keep = jnp.minimum(jnp.sum(same.astype(jnp.int32), axis=1, keepdims=True), 1)
    hot = (rank == lane).astype(jnp.int32)
    slot = jnp.sum(hot * sub, axis=0, keepdims=True)
    partner = jnp.sum(hot * other_s, axis=0, keepdims=True)
    kept = jnp.sum(hot * keep, axis=0, keepdims=True)
    upto = jnp.sum((key_s <= lane).astype(jnp.int32), axis=0, keepdims=True)
    here = jnp.sum((key_s == lane).astype(jnp.int32), axis=0, keepdims=True)
    meta[base : base + 1, :] = slot
    meta[base + 1 : base + 2, :] = partner
    meta[base + 2 : base + 3, :] = kept
    meta[base + 3 : base + 4, :] = jnp.maximum(upto - 1, 0)
    meta[base + 4 : base + 5, :] = jnp.minimum(here, 1)


def kernel(
    n_row,
    n_col,
    scale,
    x_ref,
    w_hbm,
    b_hbm,
    tiles_hbm,
    trow_hbm,
    tcol_hbm,
    count_ref,
    ct_hbm,
    out_ref,
    gf_ref,
    gw_ref,
    gb_ref,
    w_ref,
    b_ref,
    trow_ref,
    tcol_ref,
    panel,
    tiles,
    ct,
    meta_v,
    meta,
    runs,
    rs_send,
    rs_recv,
    grads,
    sib_send,
    sib_recv,
    ring_send,
    ring_recv,
    wz_send,
    wz_recv,
    wc_send,
    wc_recv,
    wx_send,
    wx_recv,
    wg_send,
    wg_recv,
    local_sem,
    ag_ss,
    ag_rs,
    sib_ss,
    sib_rs,
    col_ss,
    col_rs,
    sr_ss,
    sr_rs,
    ring_ss,
    ring_rs,
    w_ss,
    w_rs,
):
    nz = n_row // 4
    ny = n_col // 2
    cap = tiles_hbm.shape[0]
    chunk = gw_ref.shape[0] // nz
    row = lax.axis_index("row")
    col = lax.axis_index("col")
    core = row % 2
    z = (row // 2) % nz
    xh = row // (2 * nz)
    y = col // 2
    xl = col % 2

    def rid(a, dz, other=0):
        xx = xh if a == 0 else 1 - xh
        kk = core if other == 0 else 1 - core
        return (xx * nz + (z + dz + nz) % nz) * 2 + kk

    def cid(dy, dx):
        return ((y + dy + ny) % ny) * 2 + (xl + dx) % 2

    def pair(index):
        return pl.ds(2 * index, 2)

    def send(src, dst, ss, rs, to_row=None, to_col=None):
        return pltpu.make_async_remote_copy(
            src_ref=src,
            dst_ref=dst,
            send_sem=ss,
            recv_sem=rs,
            device_id={
                "row": row if to_row is None else to_row,
                "col": col if to_col is None else to_col,
            },
            device_id_type=pl.DeviceIdType.MESH,
        )

    started = []

    def go(copy):
        copy.start()
        started.append(copy)

    def drain(keep):
        for copy in started[: len(started) - keep]:
            copy.wait_send()
        del started[: len(started) - keep]

    sibling = rid(0, 0, 1)
    across = rid(1, 0)
    shifts = sorted(
        ((dy, dx) for dy in range(ny) for dx in range(2) if dy or dx),
        key=lambda p: -(min(p[0], ny - p[0]) + p[1]),
    )

    loads = [
        pltpu.make_async_copy(src, dst, local_sem.at[i])
        for i, (src, dst) in enumerate(
            (
                (trow_hbm, trow_ref),
                (tcol_hbm, tcol_ref),
                (x_ref, panel.at[pair(row)]),
                (w_hbm, w_ref),
                (b_hbm, b_ref),
                (ct_hbm, ct),
                (tiles_hbm, tiles),
            )
        )
    ]

    barrier = pltpu.get_barrier_semaphore()
    greet = [sibling, across] + [rid(0, d) for d in (1, 2, -1, -2)]
    for other in greet:
        pl.semaphore_signal(
            barrier, inc=1, device_id={"row": other, "col": col},
            device_id_type=pl.DeviceIdType.MESH,
        )
    for shift in shifts:
        pl.semaphore_signal(
            barrier, inc=1, device_id={"row": row, "col": cid(*shift)},
            device_id_type=pl.DeviceIdType.MESH,
        )
    for load in loads:
        load.start()
    pl.semaphore_wait(barrier, len(greet) + len(shifts))

    def ag(a, dz, t, to, src=None):
        k = (a * nz + dz % nz) * 2 + t
        if src is None:
            src = rid(a, dz)
        return send(
            x_ref.at[pl.ds(t, 1)] if to is not None and src is row else panel.at[pl.ds(2 * src + t, 1)],
            panel.at[pl.ds(2 * src + t, 1)],
            ag_ss.at[k],
            ag_rs.at[k],
            across if to is None else to,
        )

    def ag_wait(a, dz, t):
        ag(a, dz, t, None).wait_recv()

    def to_sibling(a, dz):
        k = a * nz + dz % nz
        blk = rid(a, dz)
        src = x_ref if a == 0 and dz == 0 else panel.at[pair(blk)]
        go(send(src, panel.at[pair(blk)], sib_ss.at[k], sib_rs.at[k], sibling))

    signs = (1, -1)
    for t in (0, 1):
        for e in signs:
            go(ag(0, -2 * e, t, rid(0, 2 * e), row))
        go(ag(1, 0, t, across, row))
    for t in (0, 1):
        for e in signs:
            go(ag(0, -e, t, rid(0, e), row))
    to_sibling(0, 0)

    for load in loads[:2]:
        load.wait()
    lane1 = lax.broadcasted_iota(jnp.int32, (1, SIDE), 1)
    live = lane1 < count_ref[0, 0]
    sort_plan(trow_ref[...], tcol_ref[...], live, meta_v, 0)
    sort_plan(tcol_ref[...], trow_ref[...], live, meta_v, 5)
    load_m = pltpu.make_async_copy(meta_v, meta, local_sem.at[7])
    load_m.start()

    for t in (0, 1):
        for e in signs:
            ag_wait(0, -2 * e, t)
            go(ag(1, -2 * e, t, across, rid(0, -2 * e)))
    for t in (0, 1):
        ag_wait(1, 0, t)
        for e in signs:
            go(ag(0, -3 * e, t, rid(0, e), rid(0, -2 * e)))
            go(ag(1, -e, t, rid(0, e), across))
    for t, e in enumerate(signs):
        go(ag(0, 4, t, rid(0, 2 * e), rid(0, -2 * e)))
    for e in signs:
        to_sibling(0, -2 * e)
    to_sibling(1, 0)
    for e in signs:
        for t in (0, 1):
            ag_wait(0, -e, t)
        to_sibling(0, -e)
    for t in (0, 1):
        for e in signs:
            ag_wait(1, -2 * e, t)
            if t == (0 if e == 1 else 1):
                go(ag(1, 4, t, rid(0, 2 * e), rid(1, -2 * e)))
            go(ag(1, -3 * e, t, rid(0, e), rid(1, -2 * e)))
    for e in signs:
        to_sibling(1, -2 * e)
    for a, dz in ((0, -3), (0, 3), (1, -1), (1, 1), (0, 4), (1, -3), (1, 3), (1, 4)):
        for t in (0, 1):
            ag_wait(a, dz, t)
        to_sibling(a, dz)
    for dz in (0, -2, 2, -1, 1, -3, 3, 4):
        for a in (0, 1):
            k = a * nz + dz % nz
            dst = panel.at[pair(rid(a, dz, 1))]
            send(dst, dst, sib_ss.at[k], sib_rs.at[k], sibling).wait_recv()
    for load in loads[2:]:
        load.wait()
    load_m.wait()

    def products(base, forward):
        def turn(i, acc):
            for u in range(UNROLL):
                s = i * UNROLL + u
                tile = tiles[meta[base, s]]
                if forward:
                    prod = jnp.dot(tile, panel[meta[base + 1, s]], preferred_element_type=F32)
                else:
                    prod = jnp.dot(grads[meta[base + 1, s]], tile, preferred_element_type=F32)
                acc = acc * meta[base + 2, s].astype(F32) + prod
                runs[s] = acc
            return acc

        lax.fori_loop(0, cap // UNROLL, turn, jnp.zeros((SIDE, SIDE), F32))

    def total(base, index):
        return runs[meta[base + 3, index]] * meta[base + 4, index].astype(F32)

    products(0, True)

    def cc(src, dst, k, to):
        return send(src, dst, col_ss.at[k], col_rs.at[k], None, to)

    for t in (0, 1):
        for j, shift in enumerate(shifts):
            i = 2 * cid(*shift) + t
            rs_send[i] = total(0, i).astype(BF16)
            mine = rs_recv.at[pl.ds(2 * col + t, 1)]
            go(cc(rs_send.at[pl.ds(i, 1)], mine, t * n_col + j, cid(*shift)))

    drain(2 * len(shifts))
    w = w_ref[...]
    agg = []
    gps = []
    outs = []
    for t in (0, 1):
        value = total(0, 2 * col + t)
        for j, (dy, dx) in reversed(list(enumerate(shifts))):
            src = cid(-dy, dx)
            i = 2 * src + t
            cc(rs_send.at[pl.ds(i, 1)], rs_recv.at[pl.ds(i, 1)], t * n_col + j, src).wait_recv()
            value = value + rs_recv[i].astype(F32)
        agg.append(value)
        hi = value.astype(BF16)
        lo = (value - hi.astype(F32)).astype(BF16)
        pre = jnp.dot(hi, w, preferred_element_type=F32) + jnp.dot(lo, w, preferred_element_type=F32)
        pre = pre + b_ref[...]
        sig = jax.nn.sigmoid(pre)
        outs.append((pre * sig).astype(BF16))
        slope = sig * (1.0 + pre * (1.0 - sig))
        gp = (ct[t * SIDE : (t + 1) * SIDE, :].astype(F32) * slope).astype(BF16)
        gps.append(gp)
        back = lax.dot_general(w, gp, (((1,), (1,)), ((), ())), preferred_element_type=F32)
        grads[2 * col + t] = back.astype(BF16)
        own = grads.at[pl.ds(2 * col + t, 1)]
        for j, shift in enumerate(shifts):
            go(cc(own, own, (2 + t) * n_col + j, cid(*shift)))

    bias = jnp.sum(gps[0].astype(F32), axis=0, keepdims=True) + jnp.sum(gps[1].astype(F32), axis=0, keepdims=True)
    dw = jnp.zeros(gw_ref.shape, F32)
    for t in (0, 1):
        turned = agg[t].T
        hi = turned.astype(BF16)
        lo = (turned - hi.astype(F32)).astype(BF16)
        dw = dw + jnp.dot(hi, gps[t], preferred_element_type=F32)
        dw = dw + jnp.dot(lo, gps[t], preferred_element_type=F32)
    bias8 = jnp.broadcast_to(bias, (8, bias.shape[1]))
    for c in range(nz):
        wz_send[c, :chunk, :] = dw[c * chunk : (c + 1) * chunk, :]
        wz_send[c, chunk:, :] = bias8
    wz_recv[z] = wz_send[z]

    def wcopy(src, dst, k, to_row=None, to_col=None):
        return send(src, dst, w_ss.at[k], w_rs.at[k], to_row, to_col)

    far = sorted(range(1, nz), key=lambda d: -min(d, nz - d))
    for d in far:
        go(wcopy(wz_send.at[(z + d) % nz], wz_recv.at[z], d, rid(0, d)))
    for t in (0, 1):
        out_ref[t * SIDE : (t + 1) * SIDE, :] = outs[t]

    drain(2 * len(shifts) + len(far))
    for t in (0, 1):
        for j, (dy, dx) in enumerate(shifts):
            src = cid(-dy, dx)
            there = grads.at[pl.ds(2 * src + t, 1)]
            cc(there, there, (2 + t) * n_col + j, src).wait_recv()

    products(5, False)

    def added(ref, n):
        value = ref[0]
        for i in range(1, n):
            value = value + ref[i]
        return value

    def over_z_done():
        for d in far:
            src = (z - d + nz) % nz
            wcopy(wz_send.at[src], wz_recv.at[src], d, rid(0, -d)).wait_recv()
        value = added(wz_recv, nz)
        wc_send[...] = value
        wc_recv[col] = value
        for j, shift in enumerate(shifts):
            go(wcopy(wc_send, wc_recv.at[col], nz + j, None, cid(*shift)))

    quad = 2 * xh + core
    quads = ((1, 1), (1, 0), (0, 1))

    def over_col_done():
        for j, (dy, dx) in enumerate(shifts):
            src = cid(-dy, dx)
            wcopy(wc_send, wc_recv.at[src], nz + j, None, src).wait_recv()
        value = added(wc_recv, n_col)
        wx_send[...] = value
        wx_recv[quad] = value
        for j, (a, other) in enumerate(quads):
            go(wcopy(wx_send, wx_recv.at[quad], nz + n_col + j, rid(a, 0, other)))

    def over_quad_done():
        for j, (a, other) in enumerate(quads):
            src = 2 * (xh if a == 0 else 1 - xh) + (core if other == 0 else 1 - core)
            wcopy(wx_send, wx_recv.at[src], nz + n_col + j, rid(a, 0, other)).wait_recv()
        value = added(wx_recv, 4) * scale
        gb_ref[...] = value[chunk : chunk + 1, :]
        wg_send[...] = value[:chunk, :].astype(BF16)
        wg_recv[z] = value[:chunk, :].astype(BF16)
        for d in far:
            go(wcopy(wg_send, wg_recv.at[z], nz + n_col + 4 + d, rid(0, d)))

    def gathered():
        for d in far:
            src = (z - d + nz) % nz
            wcopy(wg_send, wg_recv.at[src], nz + n_col + 4 + d, rid(0, -d)).wait_recv()
        for c in range(nz):
            gw_ref[c * chunk : (c + 1) * chunk, :] = wg_recv[c].astype(F32)

    order = [(1, 3), (1, -3), (1, 4), (0, 3), (0, -3), (0, 4), (1, 2), (1, -2)]
    order += [(1, 1), (1, -1), (0, 1), (0, -1), (0, 2), (0, -2), (1, 0), (0, 0)]

    def sib_copy(a, dz):
        k = a * nz + dz % nz
        return send(sib_send.at[k], sib_recv.at[k], sr_ss.at[k], sr_rs.at[k], sibling)

    for a, dz in order:
        for t in (0, 1):
            sib_send[a * nz + dz % nz, t] = total(5, 2 * rid(a, dz, 1) + t).astype(BF16)
        go(sib_copy(a, dz))
    over_z_done()

    def comb(a, dz, t):
        return total(5, 2 * rid(a, dz) + t) + sib_recv[a * nz + dz % nz, t].astype(F32)

    slots = {}
    for a in (0, 1):
        for e in signs:
            for name in ("three", "four", "one"):
                slots[name, a, e] = len(slots)
    for e in signs:
        slots["cross", 0, e] = len(slots)
        slots["two", 0, e] = len(slots)
    slots["zero", 0, 1] = len(slots)

    def ring(name, a, e, t, to):
        k = slots[name, a, e]
        return send(
            ring_send.at[k, pl.ds(t, 1)],
            ring_recv.at[k, pl.ds(t, 1)],
            ring_ss.at[2 * k + t],
            ring_rs.at[2 * k + t],
            to,
        )

    def ring_go(name, a, e, t, to, value):
        ring_send[slots[name, a, e], t] = value.astype(BF16)
        go(ring(name, a, e, t, to))

    def arrived(name, a, e, t):
        ring(name, a, e, t, across).wait_recv()
        return ring_recv[slots[name, a, e], t].astype(F32)

    for a in (1, 0):
        for e in signs:
            sib_copy(a, 3 * e).wait_recv()
            for t in (0, 1):
                ring_go("three", a, e, t, rid(0, e), comb(a, 3 * e, t))
        sib_copy(a, 4).wait_recv()
        for t, e in enumerate((-1, 1)):
            ring_go("four", a, e, t, rid(0, 2 * e), comb(a, 4, t))
    for a in (1, 0):
        for e in signs:
            sib_copy(a, e).wait_recv()
            for t in (0, 1):
                ring_go("one", a, e, t, rid(0, e), comb(a, e, t))

    drain(24)

    def near(a, e, t):
        value = comb(a, 2 * e, t) + arrived("three", a, e, t)
        if t == (0 if e == -1 else 1):
            value = value + arrived("four", a, e, t)
        return value

    for e in signs:
        sib_copy(1, 2 * e).wait_recv()
    for t in (0, 1):
        for e in signs:
            ring_go("cross", 0, e, t, across, near(1, e, t))
    over_col_done()
    sib_copy(1, 0).wait_recv()
    for t in (0, 1):
        value = comb(1, 0, t) + arrived("one", 1, 1, t) + arrived("one", 1, -1, t)
        ring_go("zero", 0, 1, t, across, value)
    for e in signs:
        sib_copy(0, 2 * e).wait_recv()
    for t in (0, 1):
        for e in signs:
            value = near(0, e, t) + arrived("cross", 0, e, t)
            ring_go("two", 0, e, t, rid(0, 2 * e), value)
    over_quad_done()
    drain(2 * len(signs) + len(far))
    sib_copy(0, 0).wait_recv()
    for t in (0, 1):
        value = comb(0, 0, t)
        for e in signs:
            value = value + arrived("one", 0, e, t)
        value = value + arrived("zero", 0, 1, t)
        for e in signs:
            value = value + arrived("two", 0, e, t)
        gf_ref[t * SIDE : (t + 1) * SIDE, :] = value.T.astype(BF16)
    gathered()
    drain(0)


def write_out(*refs):
    copies = [pltpu.make_async_copy(refs[i], refs[4 + i], refs[8].at[i]) for i in range(4)]
    for copy in copies:
        copy.start()
    for copy in copies:
        copy.wait()


def local(n_row, n_col, features, weight, bias, tile_values, tile_row, tile_col, tile_count, cotangent):
    nodes, f = features.shape
    h = weight.shape[1]
    cap = tile_values.shape[2]
    nz = n_row // 4
    chunk = f // nz
    scale = (n_row * n_col * nodes) ** (-0.5)
    pad = SIDE - tile_row.shape[-1]
    trow = jnp.pad(tile_row.reshape(1, -1), ((0, 0), (0, pad)))
    tcol = jnp.pad(tile_col.reshape(1, -1), ((0, 0), (0, pad)))
    vmem = pl.BlockSpec(memory_space=pltpu.VMEM)
    hbm = pl.BlockSpec(memory_space=pltpu.HBM)
    dma = pltpu.SemaphoreType.DMA
    square = (SIDE, SIDE)
    output, gf, gw, gb = pl.pallas_call(
        functools.partial(kernel, n_row, n_col, scale),
        out_shape=(
            jax.ShapeDtypeStruct((nodes, h), BF16),
            jax.ShapeDtypeStruct((nodes, f), BF16),
            jax.ShapeDtypeStruct((f, h), F32),
            jax.ShapeDtypeStruct((1, h), F32),
        ),
        in_specs=[hbm] * 6 + [pl.BlockSpec(memory_space=pltpu.SMEM), hbm],
        out_specs=(vmem,) * 4,
        scratch_shapes=[
            pltpu.VMEM((f, h), BF16),
            pltpu.VMEM((1, h), F32),
            pltpu.VMEM((1, SIDE), jnp.int32),
            pltpu.VMEM((1, SIDE), jnp.int32),
            pltpu.VMEM((2 * n_row,) + square, BF16),
            pltpu.VMEM((cap,) + square, BF16),
            pltpu.VMEM((nodes, h), BF16),
            pltpu.VMEM((16, SIDE), jnp.int32),
            pltpu.SMEM((16, SIDE), jnp.int32),
            pltpu.VMEM((cap,) + square, F32),
            pltpu.VMEM((2 * n_col,) + square, BF16),
            pltpu.VMEM((2 * n_col,) + square, BF16),
            pltpu.VMEM((2 * n_col,) + square, BF16),
            pltpu.VMEM((2 * nz, 2) + square, BF16),
            pltpu.VMEM((2 * nz, 2) + square, BF16),
            pltpu.VMEM((17, 2) + square, BF16),
            pltpu.VMEM((17, 2) + square, BF16),
            pltpu.VMEM((nz, chunk + 8, h), F32),
            pltpu.VMEM((nz, chunk + 8, h), F32),
            pltpu.VMEM((chunk + 8, h), F32),
            pltpu.VMEM((n_col, chunk + 8, h), F32),
            pltpu.VMEM((chunk + 8, h), F32),
            pltpu.VMEM((4, chunk + 8, h), F32),
            pltpu.VMEM((chunk, h), BF16),
            pltpu.VMEM((nz, chunk, h), BF16),
            dma((8,)),
            dma((4 * nz,)),
            dma((4 * nz,)),
            dma((2 * nz,)),
            dma((2 * nz,)),
            dma((4 * n_col,)),
            dma((4 * n_col,)),
            dma((2 * nz,)),
            dma((2 * nz,)),
            dma((34,)),
            dma((34,)),
            dma((2 * nz + n_col + 4,)),
            dma((2 * nz + n_col + 4,)),
        ],
        compiler_params=pltpu.CompilerParams(
            collective_id=0, has_side_effects=True, vmem_limit_bytes=48 * 1024 * 1024
        ),
    )(
        *(
            pltpu.with_memory_space_constraint(operand, pltpu.HBM)
            for operand in (
                features.reshape(2, SIDE, f),
                weight,
                bias.reshape(1, h),
                tile_values.reshape(tile_values.shape[2:]),
                trow,
                tcol,
            )
        ),
        tile_count,
        pltpu.with_memory_space_constraint(cotangent, pltpu.HBM),
    )
    results = (output, gf, gw, gb)
    output, gf, gw, gb = pl.pallas_call(
        write_out,
        out_shape=tuple(jax.ShapeDtypeStruct(a.shape, a.dtype) for a in results),
        in_specs=[pl.BlockSpec(memory_space=pl.ANY)] * 4,
        out_specs=(hbm,) * 4,
        scratch_shapes=[dma((4,))],
        compiler_params=pltpu.CompilerParams(vmem_limit_bytes=1024 * 1024),
    )(*(pltpu.with_memory_space_constraint(a, pltpu.VMEM) for a in results))
    return output, gf, gw, gb.reshape(h)


def solution(mesh):
    placed = (
        P(("col", "row"), None),
        P(),
        P(),
        P("row", "col", None, None, None),
        P("row", "col", None),
        P("row", "col", None),
        P("row", "col"),
        P(("row", "col"), None),
    )
    return jax.shard_map(
        functools.partial(local, mesh.shape["row"], mesh.shape["col"]),
        mesh=mesh,
        in_specs=placed,
        out_specs=(P(("row", "col"), None), P(("col", "row"), None), P(), P()),
        check_vma=False,
    )
```

```python
import functools

import jax
import jax.numpy as jnp
from jax import lax
from jax.experimental import pallas as pl
from jax.experimental.pallas import tpu as pltpu
from jax.sharding import PartitionSpec as P

F32 = jnp.float32
BF16 = jnp.bfloat16
SIDE = 128
UNROLL = 128


def sort_plan(key, other, live, meta, base):
    shape = (SIDE, SIDE)
    lane = lax.broadcasted_iota(jnp.int32, shape, 1)
    sub = lax.broadcasted_iota(jnp.int32, shape, 0)
    key_l = jnp.broadcast_to(jnp.where(live, key, SIDE), shape)
    key_s = key_l.T
    other_s = jnp.broadcast_to(other, shape).T
    less = (key_l < key_s) | ((key_l == key_s) & (lane < sub))
    rank = jnp.sum(less.astype(jnp.int32), axis=1, keepdims=True)
    same = (key_l == key_s) & (lane < sub)
    keep = jnp.minimum(jnp.sum(same.astype(jnp.int32), axis=1, keepdims=True), 1)
    hot = (rank == lane).astype(jnp.int32)
    slot = jnp.sum(hot * sub, axis=0, keepdims=True)
    partner = jnp.sum(hot * other_s, axis=0, keepdims=True)
    kept = jnp.sum(hot * keep, axis=0, keepdims=True)
    upto = jnp.sum((key_s <= lane).astype(jnp.int32), axis=0, keepdims=True)
    here = jnp.sum((key_s == lane).astype(jnp.int32), axis=0, keepdims=True)
    meta[base : base + 1, :] = slot
    meta[base + 1 : base + 2, :] = partner
    meta[base + 2 : base + 3, :] = kept
    meta[base + 3 : base + 4, :] = jnp.maximum(upto - 1, 0)
    meta[base + 4 : base + 5, :] = jnp.minimum(here, 1)


def kernel(
    n_row,
    n_col,
    scale,
    x_ref,
    w_hbm,
    b_hbm,
    tiles_hbm,
    trow_hbm,
    tcol_hbm,
    count_ref,
    ct_hbm,
    out_ref,
    gf_ref,
    gw_ref,
    gb_ref,
    w_ref,
    b_ref,
    trow_ref,
    tcol_ref,
    panel,
    tiles,
    ct,
    meta_v,
    meta,
    runs,
    rs_send,
    rs_recv,
    grads,
    sib_send,
    sib_recv,
    ring_send,
    ring_recv,
    wz_send,
    wz_recv,
    wc_send,
    wc_recv,
    wx_send,
    wx_recv,
    wg_send,
    wg_recv,
    local_sem,
    ag_ss,
    ag_rs,
    sib_ss,
    sib_rs,
    col_ss,
    col_rs,
    sr_ss,
    sr_rs,
    ring_ss,
    ring_rs,
    w_ss,
    w_rs,
):
    nz = n_row // 4
    ny = n_col // 2
    cap = tiles_hbm.shape[0]
    chunk = gw_ref.shape[0] // nz
    row = lax.axis_index("row")
    col = lax.axis_index("col")
    core = row % 2
    z = (row // 2) % nz
    xh = row // (2 * nz)
    y = col // 2
    xl = col % 2

    def rid(a, dz, other=0):
        xx = xh if a == 0 else 1 - xh
        kk = core if other == 0 else 1 - core
        return (xx * nz + (z + dz + nz) % nz) * 2 + kk

    def cid(dy, dx):
        return ((y + dy + ny) % ny) * 2 + (xl + dx) % 2

    def pair(index):
        return pl.ds(2 * index, 2)

    def send(src, dst, ss, rs, to_row=None, to_col=None):
        return pltpu.make_async_remote_copy(
            src_ref=src,
            dst_ref=dst,
            send_sem=ss,
            recv_sem=rs,
            device_id={
                "row": row if to_row is None else to_row,
                "col": col if to_col is None else to_col,
            },
            device_id_type=pl.DeviceIdType.MESH,
        )

    started = []

    def go(copy):
        copy.start()
        started.append(copy)

    def drain(keep):
        for copy in started[: len(started) - keep]:
            copy.wait_send()
        del started[: len(started) - keep]

    sibling = rid(0, 0, 1)
    across = rid(1, 0)
    shifts = sorted(
        ((dy, dx) for dy in range(ny) for dx in range(2) if dy or dx),
        key=lambda p: -(min(p[0], ny - p[0]) + p[1]),
    )

    loads = [
        pltpu.make_async_copy(src, dst, local_sem.at[i])
        for i, (src, dst) in enumerate(
            (
                (trow_hbm, trow_ref),
                (tcol_hbm, tcol_ref),
                (x_ref, panel.at[pair(row)]),
                (w_hbm, w_ref),
                (b_hbm, b_ref),
                (ct_hbm, ct),
                (tiles_hbm, tiles),
            )
        )
    ]

    barrier = pltpu.get_barrier_semaphore()
    greet = [sibling, across] + [rid(0, d) for d in (1, 2, -1, -2)]
    for other in greet:
        pl.semaphore_signal(
            barrier, inc=1, device_id={"row": other, "col": col},
            device_id_type=pl.DeviceIdType.MESH,
        )
    for shift in shifts:
        pl.semaphore_signal(
            barrier, inc=1, device_id={"row": row, "col": cid(*shift)},
            device_id_type=pl.DeviceIdType.MESH,
        )
    for load in loads:
        load.start()
    pl.semaphore_wait(barrier, len(greet) + len(shifts))

    def ag(a, dz, t, to, src=None):
        k = (a * nz + dz % nz) * 2 + t
        if src is None:
            src = rid(a, dz)
        return send(
            x_ref.at[pl.ds(t, 1)] if to is not None and src is row else panel.at[pl.ds(2 * src + t, 1)],
            panel.at[pl.ds(2 * src + t, 1)],
            ag_ss.at[k],
            ag_rs.at[k],
            across if to is None else to,
        )

    def ag_wait(a, dz, t):
        ag(a, dz, t, None).wait_recv()

    def to_sibling(a, dz):
        k = a * nz + dz % nz
        blk = rid(a, dz)
        src = x_ref if a == 0 and dz == 0 else panel.at[pair(blk)]
        go(send(src, panel.at[pair(blk)], sib_ss.at[k], sib_rs.at[k], sibling))

    signs = (1, -1)
    for t in (0, 1):
        for e in signs:
            go(ag(0, -2 * e, t, rid(0, 2 * e), row))
        go(ag(1, 0, t, across, row))
    for t in (0, 1):
        for e in signs:
            go(ag(0, -e, t, rid(0, e), row))
    to_sibling(0, 0)

    for load in loads[:2]:
        load.wait()
    lane1 = lax.broadcasted_iota(jnp.int32, (1, SIDE), 1)
    live = lane1 < count_ref[0, 0]
    sort_plan(trow_ref[...], tcol_ref[...], live, meta_v, 0)
    sort_plan(tcol_ref[...], trow_ref[...], live, meta_v, 5)
    load_m = pltpu.make_async_copy(meta_v, meta, local_sem.at[7])
    load_m.start()

    for t in (0, 1):
        for e in signs:
            ag_wait(0, -2 * e, t)
            go(ag(1, -2 * e, t, across, rid(0, -2 * e)))
    for t in (0, 1):
        ag_wait(1, 0, t)
        for e in signs:
            go(ag(0, -3 * e, t, rid(0, e), rid(0, -2 * e)))
            go(ag(1, -e, t, rid(0, e), across))
    for t, e in enumerate(signs):
        go(ag(0, 4, t, rid(0, 2 * e), rid(0, -2 * e)))
    for e in signs:
        to_sibling(0, -2 * e)
    to_sibling(1, 0)
    for e in signs:
        for t in (0, 1):
            ag_wait(0, -e, t)
        to_sibling(0, -e)
    for t in (0, 1):
        for e in signs:
            ag_wait(1, -2 * e, t)
            if t == (0 if e == 1 else 1):
                go(ag(1, 4, t, rid(0, 2 * e), rid(1, -2 * e)))
            go(ag(1, -3 * e, t, rid(0, e), rid(1, -2 * e)))
    for e in signs:
        to_sibling(1, -2 * e)
    for a, dz in ((0, -3), (0, 3), (1, -1), (1, 1), (0, 4), (1, -3), (1, 3), (1, 4)):
        for t in (0, 1):
            ag_wait(a, dz, t)
        to_sibling(a, dz)
    for dz in (0, -2, 2, -1, 1, -3, 3, 4):
        for a in (0, 1):
            k = a * nz + dz % nz
            dst = panel.at[pair(rid(a, dz, 1))]
            send(dst, dst, sib_ss.at[k], sib_rs.at[k], sibling).wait_recv()
    for load in loads[2:]:
        load.wait()
    load_m.wait()

    def products(base, forward):
        def turn(i, acc):
            for u in range(UNROLL):
                s = i * UNROLL + u
                tile = tiles[meta[base, s]]
                if forward:
                    prod = jnp.dot(tile, panel[meta[base + 1, s]], preferred_element_type=F32)
                else:
                    prod = jnp.dot(grads[meta[base + 1, s]], tile, preferred_element_type=F32)
                acc = acc * meta[base + 2, s].astype(F32) + prod
                runs[s] = acc
            return acc

        lax.fori_loop(0, cap // UNROLL, turn, jnp.zeros((SIDE, SIDE), F32))

    def total(base, index):
        return runs[meta[base + 3, index]] * meta[base + 4, index].astype(F32)

    products(0, True)

    def cc(src, dst, k, to):
        return send(src, dst, col_ss.at[k], col_rs.at[k], None, to)

    for t in (0, 1):
        for j, shift in enumerate(shifts):
            i = 2 * cid(*shift) + t
            rs_send[i] = total(0, i).astype(BF16)
            mine = rs_recv.at[pl.ds(2 * col + t, 1)]
            go(cc(rs_send.at[pl.ds(i, 1)], mine, t * n_col + j, cid(*shift)))

    drain(2 * len(shifts))
    w = w_ref[...]
    agg = []
    gps = []
    outs = []
    for t in (0, 1):
        value = total(0, 2 * col + t)
        for j, (dy, dx) in reversed(list(enumerate(shifts))):
            src = cid(-dy, dx)
            i = 2 * src + t
            cc(rs_send.at[pl.ds(i, 1)], rs_recv.at[pl.ds(i, 1)], t * n_col + j, src).wait_recv()
            value = value + rs_recv[i].astype(F32)
        agg.append(value)
        hi = value.astype(BF16)
        lo = (value - hi.astype(F32)).astype(BF16)
        pre = jnp.dot(hi, w, preferred_element_type=F32) + jnp.dot(lo, w, preferred_element_type=F32)
        pre = pre + b_ref[...]
        sig = jax.nn.sigmoid(pre)
        outs.append((pre * sig).astype(BF16))
        slope = sig * (1.0 + pre * (1.0 - sig))
        gp = (ct[t * SIDE : (t + 1) * SIDE, :].astype(F32) * slope).astype(BF16)
        gps.append(gp)
        back = lax.dot_general(w, gp, (((1,), (1,)), ((), ())), preferred_element_type=F32)
        grads[2 * col + t] = back.astype(BF16)
        own = grads.at[pl.ds(2 * col + t, 1)]
        for j, shift in enumerate(shifts):
            go(cc(own, own, (2 + t) * n_col + j, cid(*shift)))

    bias = jnp.sum(gps[0].astype(F32), axis=0, keepdims=True) + jnp.sum(gps[1].astype(F32), axis=0, keepdims=True)
    dw = jnp.zeros(gw_ref.shape, F32)
    for t in (0, 1):
        turned = agg[t].T
        hi = turned.astype(BF16)
        lo = (turned - hi.astype(F32)).astype(BF16)
        dw = dw + jnp.dot(hi, gps[t], preferred_element_type=F32)
        dw = dw + jnp.dot(lo, gps[t], preferred_element_type=F32)
    bias8 = jnp.broadcast_to(bias, (8, bias.shape[1]))
    for c in range(nz):
        wz_send[c, :chunk, :] = dw[c * chunk : (c + 1) * chunk, :]
        wz_send[c, chunk:, :] = bias8
    wz_recv[z] = wz_send[z]

    def wcopy(src, dst, k, to_row=None, to_col=None):
        return send(src, dst, w_ss.at[k], w_rs.at[k], to_row, to_col)

    far = sorted(range(1, nz), key=lambda d: -min(d, nz - d))
    for d in far:
        go(wcopy(wz_send.at[(z + d) % nz], wz_recv.at[z], d, rid(0, d)))
    for t in (0, 1):
        out_ref[t * SIDE : (t + 1) * SIDE, :] = outs[t]

    drain(2 * len(shifts) + len(far))
    for t in (0, 1):
        for j, (dy, dx) in enumerate(shifts):
            src = cid(-dy, dx)
            there = grads.at[pl.ds(2 * src + t, 1)]
            cc(there, there, (2 + t) * n_col + j, src).wait_recv()

    products(5, False)

    def added(ref, n):
        value = ref[0]
        for i in range(1, n):
            value = value + ref[i]
        return value

    def over_z_done():
        for d in far:
            src = (z - d + nz) % nz
            wcopy(wz_send.at[src], wz_recv.at[src], d, rid(0, -d)).wait_recv()
        value = added(wz_recv, nz)
        wc_send[...] = value
        wc_recv[col] = value
        for j, shift in enumerate(shifts):
            go(wcopy(wc_send, wc_recv.at[col], nz + j, None, cid(*shift)))

    quad = 2 * xh + core
    quads = ((1, 1), (1, 0), (0, 1))

    def over_col_done():
        for j, (dy, dx) in enumerate(shifts):
            src = cid(-dy, dx)
            wcopy(wc_send, wc_recv.at[src], nz + j, None, src).wait_recv()
        value = added(wc_recv, n_col)
        wx_send[...] = value
        wx_recv[quad] = value
        for j, (a, other) in enumerate(quads):
            go(wcopy(wx_send, wx_recv.at[quad], nz + n_col + j, rid(a, 0, other)))

    def over_quad_done():
        for j, (a, other) in enumerate(quads):
            src = 2 * (xh if a == 0 else 1 - xh) + (core if other == 0 else 1 - core)
            wcopy(wx_send, wx_recv.at[src], nz + n_col + j, rid(a, 0, other)).wait_recv()
        value = added(wx_recv, 4) * scale
        gb_ref[...] = value[chunk : chunk + 1, :]
        wg_send[...] = value[:chunk, :].astype(BF16)
        wg_recv[z] = value[:chunk, :].astype(BF16)
        for d in far:
            go(wcopy(wg_send, wg_recv.at[z], nz + n_col + 4 + d, rid(0, d)))

    def gathered():
        for d in far:
            src = (z - d + nz) % nz
            wcopy(wg_send, wg_recv.at[src], nz + n_col + 4 + d, rid(0, -d)).wait_recv()
        for c in range(nz):
            gw_ref[c * chunk : (c + 1) * chunk, :] = wg_recv[c].astype(F32)

    order = [(1, 3), (1, -3), (1, 4), (1, 2), (1, -2), (1, 1), (1, -1), (0, 3), (0, -3), (0, 4)]
    order += [(1, 0), (0, 1), (0, -1), (0, 2), (0, -2), (0, 0)]

    def sib_copy(a, dz):
        k = a * nz + dz % nz
        return send(sib_send.at[k], sib_recv.at[k], sr_ss.at[k], sr_rs.at[k], sibling)

    for a, dz in order:
        for t in (0, 1):
            sib_send[a * nz + dz % nz, t] = total(5, 2 * rid(a, dz, 1) + t).astype(BF16)
        go(sib_copy(a, dz))
    over_z_done()

    def comb(a, dz, t):
        return total(5, 2 * rid(a, dz) + t) + sib_recv[a * nz + dz % nz, t].astype(F32)

    slots = {}
    for a in (0, 1):
        for e in signs:
            for name in ("three", "four", "one"):
                slots[name, a, e] = len(slots)
    for e in signs:
        slots["cross", 0, e] = len(slots)
        slots["two", 0, e] = len(slots)
    slots["zero", 0, 1] = len(slots)

    def ring(name, a, e, t, to):
        k = slots[name, a, e]
        return send(
            ring_send.at[k, pl.ds(t, 1)],
            ring_recv.at[k, pl.ds(t, 1)],
            ring_ss.at[2 * k + t],
            ring_rs.at[2 * k + t],
            to,
        )

    def ring_go(name, a, e, t, to, value):
        ring_send[slots[name, a, e], t] = value.astype(BF16)
        go(ring(name, a, e, t, to))

    def arrived(name, a, e, t):
        ring(name, a, e, t, across).wait_recv()
        return ring_recv[slots[name, a, e], t].astype(F32)

    for a in (1,):
        for e in signs:
            sib_copy(a, 3 * e).wait_recv()
            for t in (0, 1):
                ring_go("three", a, e, t, rid(0, e), comb(a, 3 * e, t))
        sib_copy(a, 4).wait_recv()
        for t, e in enumerate((-1, 1)):
            ring_go("four", a, e, t, rid(0, 2 * e), comb(a, 4, t))
    for a in (1,):
        for e in signs:
            sib_copy(a, e).wait_recv()
            for t in (0, 1):
                ring_go("one", a, e, t, rid(0, e), comb(a, e, t))
    for a in (0,):
        for e in signs:
            sib_copy(a, 3 * e).wait_recv()
            for t in (0, 1):
                ring_go("three", a, e, t, rid(0, e), comb(a, 3 * e, t))
        sib_copy(a, 4).wait_recv()
        for t, e in enumerate((-1, 1)):
            ring_go("four", a, e, t, rid(0, 2 * e), comb(a, 4, t))
    for a in (0,):
        for e in signs:
            sib_copy(a, e).wait_recv()
            for t in (0, 1):
                ring_go("one", a, e, t, rid(0, e), comb(a, e, t))

    drain(24)

    def near(a, e, t):
        value = comb(a, 2 * e, t) + arrived("three", a, e, t)
        if t == (0 if e == -1 else 1):
            value = value + arrived("four", a, e, t)
        return value

    for e in signs:
        sib_copy(1, 2 * e).wait_recv()
    for t in (0, 1):
        for e in signs:
            ring_go("cross", 0, e, t, across, near(1, e, t))
    over_col_done()
    sib_copy(1, 0).wait_recv()
    for t in (0, 1):
        value = comb(1, 0, t) + arrived("one", 1, 1, t) + arrived("one", 1, -1, t)
        ring_go("zero", 0, 1, t, across, value)
    for e in signs:
        sib_copy(0, 2 * e).wait_recv()
    for t in (0, 1):
        for e in signs:
            value = near(0, e, t) + arrived("cross", 0, e, t)
            ring_go("two", 0, e, t, rid(0, 2 * e), value)
    over_quad_done()
    drain(2 * len(signs) + len(far))
    sib_copy(0, 0).wait_recv()
    for t in (0, 1):
        value = comb(0, 0, t)
        for e in signs:
            value = value + arrived("one", 0, e, t)
        value = value + arrived("zero", 0, 1, t)
        for e in signs:
            value = value + arrived("two", 0, e, t)
        gf_ref[t * SIDE : (t + 1) * SIDE, :] = value.T.astype(BF16)
    gathered()
    drain(0)


def write_out(*refs):
    copies = [pltpu.make_async_copy(refs[i], refs[4 + i], refs[8].at[i]) for i in range(4)]
    for copy in copies:
        copy.start()
    for copy in copies:
        copy.wait()


def local(n_row, n_col, features, weight, bias, tile_values, tile_row, tile_col, tile_count, cotangent):
    nodes, f = features.shape
    h = weight.shape[1]
    cap = tile_values.shape[2]
    nz = n_row // 4
    chunk = f // nz
    scale = (n_row * n_col * nodes) ** (-0.5)
    pad = SIDE - tile_row.shape[-1]
    trow = jnp.pad(tile_row.reshape(1, -1), ((0, 0), (0, pad)))
    tcol = jnp.pad(tile_col.reshape(1, -1), ((0, 0), (0, pad)))
    vmem = pl.BlockSpec(memory_space=pltpu.VMEM)
    hbm = pl.BlockSpec(memory_space=pltpu.HBM)
    dma = pltpu.SemaphoreType.DMA
    square = (SIDE, SIDE)
    output, gf, gw, gb = pl.pallas_call(
        functools.partial(kernel, n_row, n_col, scale),
        out_shape=(
            jax.ShapeDtypeStruct((nodes, h), BF16),
            jax.ShapeDtypeStruct((nodes, f), BF16),
            jax.ShapeDtypeStruct((f, h), F32),
            jax.ShapeDtypeStruct((1, h), F32),
        ),
        in_specs=[hbm] * 6 + [pl.BlockSpec(memory_space=pltpu.SMEM), hbm],
        out_specs=(vmem,) * 4,
        scratch_shapes=[
            pltpu.VMEM((f, h), BF16),
            pltpu.VMEM((1, h), F32),
            pltpu.VMEM((1, SIDE), jnp.int32),
            pltpu.VMEM((1, SIDE), jnp.int32),
            pltpu.VMEM((2 * n_row,) + square, BF16),
            pltpu.VMEM((cap,) + square, BF16),
            pltpu.VMEM((nodes, h), BF16),
            pltpu.VMEM((16, SIDE), jnp.int32),
            pltpu.SMEM((16, SIDE), jnp.int32),
            pltpu.VMEM((cap,) + square, F32),
            pltpu.VMEM((2 * n_col,) + square, BF16),
            pltpu.VMEM((2 * n_col,) + square, BF16),
            pltpu.VMEM((2 * n_col,) + square, BF16),
            pltpu.VMEM((2 * nz, 2) + square, BF16),
            pltpu.VMEM((2 * nz, 2) + square, BF16),
            pltpu.VMEM((17, 2) + square, BF16),
            pltpu.VMEM((17, 2) + square, BF16),
            pltpu.VMEM((nz, chunk + 8, h), F32),
            pltpu.VMEM((nz, chunk + 8, h), F32),
            pltpu.VMEM((chunk + 8, h), F32),
            pltpu.VMEM((n_col, chunk + 8, h), F32),
            pltpu.VMEM((chunk + 8, h), F32),
            pltpu.VMEM((4, chunk + 8, h), F32),
            pltpu.VMEM((chunk, h), BF16),
            pltpu.VMEM((nz, chunk, h), BF16),
            dma((8,)),
            dma((4 * nz,)),
            dma((4 * nz,)),
            dma((2 * nz,)),
            dma((2 * nz,)),
            dma((4 * n_col,)),
            dma((4 * n_col,)),
            dma((2 * nz,)),
            dma((2 * nz,)),
            dma((34,)),
            dma((34,)),
            dma((2 * nz + n_col + 4,)),
            dma((2 * nz + n_col + 4,)),
        ],
        compiler_params=pltpu.CompilerParams(
            collective_id=0, has_side_effects=True, vmem_limit_bytes=48 * 1024 * 1024
        ),
    )(
        *(
            pltpu.with_memory_space_constraint(operand, pltpu.HBM)
            for operand in (
                features.reshape(2, SIDE, f),
                weight,
                bias.reshape(1, h),
                tile_values.reshape(tile_values.shape[2:]),
                trow,
                tcol,
            )
        ),
        tile_count,
        pltpu.with_memory_space_constraint(cotangent, pltpu.HBM),
    )
    results = (output, gf, gw, gb)
    output, gf, gw, gb = pl.pallas_call(
        write_out,
        out_shape=tuple(jax.ShapeDtypeStruct(a.shape, a.dtype) for a in results),
        in_specs=[pl.BlockSpec(memory_space=pl.ANY)] * 4,
        out_specs=(hbm,) * 4,
        scratch_shapes=[dma((4,))],
        compiler_params=pltpu.CompilerParams(vmem_limit_bytes=1024 * 1024),
    )(*(pltpu.with_memory_space_constraint(a, pltpu.VMEM) for a in results))
    return output, gf, gw, gb.reshape(h)


def solution(mesh):
    placed = (
        P(("col", "row"), None),
        P(),
        P(),
        P("row", "col", None, None, None),
        P("row", "col", None),
        P("row", "col", None),
        P("row", "col"),
        P(("row", "col"), None),
    )
    return jax.shard_map(
        functools.partial(local, mesh.shape["row"], mesh.shape["col"]),
        mesh=mesh,
        in_specs=placed,
        out_specs=(P(("row", "col"), None), P(("col", "row"), None), P(), P()),
        check_vma=False,
    )
```

```python
import functools

import jax
import jax.numpy as jnp
from jax import lax
from jax.experimental import pallas as pl
from jax.experimental.pallas import tpu as pltpu
from jax.sharding import PartitionSpec as P

F32 = jnp.float32
BF16 = jnp.bfloat16
SIDE = 128
UNROLL = 128


def sort_plan(key, other, live, meta, base):
    shape = (SIDE, SIDE)
    lane = lax.broadcasted_iota(jnp.int32, shape, 1)
    sub = lax.broadcasted_iota(jnp.int32, shape, 0)
    key_l = jnp.broadcast_to(jnp.where(live, key, SIDE), shape)
    key_s = key_l.T
    other_s = jnp.broadcast_to(other, shape).T
    less = (key_l < key_s) | ((key_l == key_s) & (lane < sub))
    rank = jnp.sum(less.astype(jnp.int32), axis=1, keepdims=True)
    same = (key_l == key_s) & (lane < sub)
    keep = jnp.minimum(jnp.sum(same.astype(jnp.int32), axis=1, keepdims=True), 1)
    hot = (rank == lane).astype(jnp.int32)
    slot = jnp.sum(hot * sub, axis=0, keepdims=True)
    partner = jnp.sum(hot * other_s, axis=0, keepdims=True)
    kept = jnp.sum(hot * keep, axis=0, keepdims=True)
    upto = jnp.sum((key_s <= lane).astype(jnp.int32), axis=0, keepdims=True)
    here = jnp.sum((key_s == lane).astype(jnp.int32), axis=0, keepdims=True)
    meta[base : base + 1, :] = slot
    meta[base + 1 : base + 2, :] = partner
    meta[base + 2 : base + 3, :] = kept
    meta[base + 3 : base + 4, :] = jnp.maximum(upto - 1, 0)
    meta[base + 4 : base + 5, :] = jnp.minimum(here, 1)


def kernel(
    n_row,
    n_col,
    scale,
    x_ref,
    w_hbm,
    b_hbm,
    tiles_hbm,
    trow_hbm,
    tcol_hbm,
    count_ref,
    ct_hbm,
    out_ref,
    gf_ref,
    gw_ref,
    gb_ref,
    w_ref,
    b_ref,
    trow_ref,
    tcol_ref,
    panel,
    tiles,
    ct,
    meta_v,
    meta,
    runs,
    rs_send,
    rs_recv,
    grads,
    sib_send,
    sib_recv,
    ring_send,
    ring_recv,
    wz_send,
    wz_recv,
    wc_send,
    wc_recv,
    wx_send,
    wx_recv,
    wg_send,
    wg_recv,
    local_sem,
    ag_ss,
    ag_rs,
    sib_ss,
    sib_rs,
    col_ss,
    col_rs,
    sr_ss,
    sr_rs,
    ring_ss,
    ring_rs,
    w_ss,
    w_rs,
):
    nz = n_row // 4
    ny = n_col // 2
    cap = tiles_hbm.shape[0]
    chunk = gw_ref.shape[0] // nz
    row = lax.axis_index("row")
    col = lax.axis_index("col")
    core = row % 2
    z = (row // 2) % nz
    xh = row // (2 * nz)
    y = col // 2
    xl = col % 2

    def rid(a, dz, other=0):
        xx = xh if a == 0 else 1 - xh
        kk = core if other == 0 else 1 - core
        return (xx * nz + (z + dz + nz) % nz) * 2 + kk

    def cid(dy, dx):
        return ((y + dy + ny) % ny) * 2 + (xl + dx) % 2

    def pair(index):
        return pl.ds(2 * index, 2)

    def send(src, dst, ss, rs, to_row=None, to_col=None):
        return pltpu.make_async_remote_copy(
            src_ref=src,
            dst_ref=dst,
            send_sem=ss,
            recv_sem=rs,
            device_id={
                "row": row if to_row is None else to_row,
                "col": col if to_col is None else to_col,
            },
            device_id_type=pl.DeviceIdType.MESH,
        )

    started = []

    def go(copy):
        copy.start()
        started.append(copy)

    def drain(keep):
        for copy in started[: len(started) - keep]:
            copy.wait_send()
        del started[: len(started) - keep]

    sibling = rid(0, 0, 1)
    across = rid(1, 0)
    shifts = sorted(
        ((dy, dx) for dy in range(ny) for dx in range(2) if dy or dx),
        key=lambda p: -(min(p[0], ny - p[0]) + p[1]),
    )

    loads = [
        pltpu.make_async_copy(src, dst, local_sem.at[i])
        for i, (src, dst) in enumerate(
            (
                (trow_hbm, trow_ref),
                (tcol_hbm, tcol_ref),
                (x_ref, panel.at[pair(row)]),
                (w_hbm, w_ref),
                (b_hbm, b_ref),
                (ct_hbm, ct),
                (tiles_hbm, tiles),
            )
        )
    ]

    barrier = pltpu.get_barrier_semaphore()
    greet = [sibling, across] + [rid(0, d) for d in (1, 2, -1, -2)]
    for other in greet:
        pl.semaphore_signal(
            barrier, inc=1, device_id={"row": other, "col": col},
            device_id_type=pl.DeviceIdType.MESH,
        )
    for shift in shifts:
        pl.semaphore_signal(
            barrier, inc=1, device_id={"row": row, "col": cid(*shift)},
            device_id_type=pl.DeviceIdType.MESH,
        )
    for load in loads:
        load.start()
    pl.semaphore_wait(barrier, len(greet) + len(shifts))

    def ag(a, dz, t, to, src=None):
        k = (a * nz + dz % nz) * 2 + t
        if src is None:
            src = rid(a, dz)
        return send(
            x_ref.at[pl.ds(t, 1)] if to is not None and src is row else panel.at[pl.ds(2 * src + t, 1)],
            panel.at[pl.ds(2 * src + t, 1)],
            ag_ss.at[k],
            ag_rs.at[k],
            across if to is None else to,
        )

    def ag_wait(a, dz, t):
        ag(a, dz, t, None).wait_recv()

    def to_sibling(a, dz):
        k = a * nz + dz % nz
        blk = rid(a, dz)
        src = x_ref if a == 0 and dz == 0 else panel.at[pair(blk)]
        go(send(src, panel.at[pair(blk)], sib_ss.at[k], sib_rs.at[k], sibling))

    signs = (1, -1)
    for t in (0, 1):
        for e in signs:
            go(ag(0, -2 * e, t, rid(0, 2 * e), row))
        go(ag(1, 0, t, across, row))
    for t in (0, 1):
        for e in signs:
            go(ag(0, -e, t, rid(0, e), row))
    to_sibling(0, 0)

    for load in loads[:2]:
        load.wait()
    lane1 = lax.broadcasted_iota(jnp.int32, (1, SIDE), 1)
    live = lane1 < count_ref[0, 0]
    sort_plan(trow_ref[...], tcol_ref[...], live, meta_v, 0)
    sort_plan(tcol_ref[...], trow_ref[...], live, meta_v, 5)
    load_m = pltpu.make_async_copy(meta_v, meta, local_sem.at[7])
    load_m.start()

    for t in (0, 1):
        for e in signs:
            ag_wait(0, -2 * e, t)
            go(ag(1, -2 * e, t, across, rid(0, -2 * e)))
    for t in (0, 1):
        ag_wait(1, 0, t)
        for e in signs:
            go(ag(0, -3 * e, t, rid(0, e), rid(0, -2 * e)))
            go(ag(1, -e, t, rid(0, e), across))
    for t, e in enumerate(signs):
        go(ag(0, 4, t, rid(0, 2 * e), rid(0, -2 * e)))
    for e in signs:
        to_sibling(0, -2 * e)
    to_sibling(1, 0)
    for e in signs:
        for t in (0, 1):
            ag_wait(0, -e, t)
        to_sibling(0, -e)
    for t in (0, 1):
        for e in signs:
            ag_wait(1, -2 * e, t)
            if t == (0 if e == 1 else 1):
                go(ag(1, 4, t, rid(0, 2 * e), rid(1, -2 * e)))
            go(ag(1, -3 * e, t, rid(0, e), rid(1, -2 * e)))
    for e in signs:
        to_sibling(1, -2 * e)
    for a, dz in ((0, -3), (0, 3), (1, -1), (1, 1), (0, 4), (1, -3), (1, 3), (1, 4)):
        for t in (0, 1):
            ag_wait(a, dz, t)
        to_sibling(a, dz)
    for dz in (0, -2, 2, -1, 1, -3, 3, 4):
        for a in (0, 1):
            k = a * nz + dz % nz
            dst = panel.at[pair(rid(a, dz, 1))]
            send(dst, dst, sib_ss.at[k], sib_rs.at[k], sibling).wait_recv()
    for load in loads[2:]:
        load.wait()
    load_m.wait()

    def products(base, forward):
        def turn(i, acc):
            for u in range(UNROLL):
                s = i * UNROLL + u
                tile = tiles[meta[base, s]]
                if forward:
                    prod = jnp.dot(tile, panel[meta[base + 1, s]], preferred_element_type=F32)
                else:
                    prod = jnp.dot(grads[meta[base + 1, s]], tile, preferred_element_type=F32)
                acc = acc * meta[base + 2, s].astype(F32) + prod
                runs[s] = acc
            return acc

        lax.fori_loop(0, cap // UNROLL, turn, jnp.zeros((SIDE, SIDE), F32))

    def total(base, index):
        return runs[meta[base + 3, index]] * meta[base + 4, index].astype(F32)

    products(0, True)

    def cc(src, dst, k, to):
        return send(src, dst, col_ss.at[k], col_rs.at[k], None, to)

    for t in (0, 1):
        for j, shift in enumerate(shifts):
            i = 2 * cid(*shift) + t
            rs_send[i] = total(0, i).astype(BF16)
            mine = rs_recv.at[pl.ds(2 * col + t, 1)]
            go(cc(rs_send.at[pl.ds(i, 1)], mine, t * n_col + j, cid(*shift)))

    drain(2 * len(shifts))
    w = w_ref[...]
    agg = []
    gps = []
    outs = []
    for t in (0, 1):
        value = total(0, 2 * col + t)
        for j, (dy, dx) in reversed(list(enumerate(shifts))):
            src = cid(-dy, dx)
            i = 2 * src + t
            cc(rs_send.at[pl.ds(i, 1)], rs_recv.at[pl.ds(i, 1)], t * n_col + j, src).wait_recv()
            value = value + rs_recv[i].astype(F32)
        agg.append(value)
        hi = value.astype(BF16)
        lo = (value - hi.astype(F32)).astype(BF16)
        pre = jnp.dot(hi, w, preferred_element_type=F32) + jnp.dot(lo, w, preferred_element_type=F32)
        pre = pre + b_ref[...]
        sig = jax.nn.sigmoid(pre)
        outs.append((pre * sig).astype(BF16))
        slope = sig * (1.0 + pre * (1.0 - sig))
        gp = (ct[t * SIDE : (t + 1) * SIDE, :].astype(F32) * slope).astype(BF16)
        gps.append(gp)
        back = lax.dot_general(w, gp, (((1,), (1,)), ((), ())), preferred_element_type=F32)
        grads[2 * col + t] = back.astype(BF16)
        own = grads.at[pl.ds(2 * col + t, 1)]
        for j, shift in enumerate(shifts):
            go(cc(own, own, (2 + t) * n_col + j, cid(*shift)))

    bias = jnp.sum(gps[0].astype(F32), axis=0, keepdims=True) + jnp.sum(gps[1].astype(F32), axis=0, keepdims=True)
    dw = jnp.zeros(gw_ref.shape, F32)
    for t in (0, 1):
        turned = agg[t].T
        hi = turned.astype(BF16)
        lo = (turned - hi.astype(F32)).astype(BF16)
        dw = dw + jnp.dot(hi, gps[t], preferred_element_type=F32)
        dw = dw + jnp.dot(lo, gps[t], preferred_element_type=F32)
    bias8 = jnp.broadcast_to(bias, (8, bias.shape[1]))
    for c in range(nz):
        wz_send[c, :chunk, :] = dw[c * chunk : (c + 1) * chunk, :]
        wz_send[c, chunk:, :] = bias8
    wz_recv[z] = wz_send[z]

    def wcopy(src, dst, k, to_row=None, to_col=None):
        return send(src, dst, w_ss.at[k], w_rs.at[k], to_row, to_col)

    far = sorted(range(1, nz), key=lambda d: -min(d, nz - d))
    for d in far:
        go(wcopy(wz_send.at[(z + d) % nz], wz_recv.at[z], d, rid(0, d)))
    for t in (0, 1):
        out_ref[t * SIDE : (t + 1) * SIDE, :] = outs[t]

    drain(2 * len(shifts) + len(far))
    for t in (0, 1):
        for j, (dy, dx) in enumerate(shifts):
            src = cid(-dy, dx)
            there = grads.at[pl.ds(2 * src + t, 1)]
            cc(there, there, (2 + t) * n_col + j, src).wait_recv()

    products(5, False)

    def added(ref, n):
        value = ref[0].astype(F32)
        for i in range(1, n):
            value = value + ref[i].astype(F32)
        return value

    def over_z_done():
        for d in far:
            src = (z - d + nz) % nz
            wcopy(wz_send.at[src], wz_recv.at[src], d, rid(0, -d)).wait_recv()
        value = added(wz_recv, nz)
        wc_send[...] = value
        wc_recv[col] = value
        for j, shift in enumerate(shifts):
            go(wcopy(wc_send, wc_recv.at[col], nz + j, None, cid(*shift)))

    quad = 2 * xh + core
    quads = ((1, 1), (1, 0), (0, 1))

    def over_col_done():
        for j, (dy, dx) in enumerate(shifts):
            src = cid(-dy, dx)
            wcopy(wc_send, wc_recv.at[src], nz + j, None, src).wait_recv()
        value = added(wc_recv, n_col)
        wx_send[...] = jnp.concatenate([value, value[chunk:, :]], axis=0).astype(BF16)
        wx_recv[quad] = wx_send[...]
        for j, (a, other) in enumerate(quads):
            go(wcopy(wx_send, wx_recv.at[quad], nz + n_col + j, rid(a, 0, other)))

    def over_quad_done():
        for j, (a, other) in enumerate(quads):
            src = 2 * (xh if a == 0 else 1 - xh) + (core if other == 0 else 1 - core)
            wcopy(wx_send, wx_recv.at[src], nz + n_col + j, rid(a, 0, other)).wait_recv()
        value = added(wx_recv, 4) * scale
        gb_ref[...] = value[chunk : chunk + 1, :]
        wg_send[...] = value[:chunk, :].astype(BF16)
        wg_recv[z] = value[:chunk, :].astype(BF16)
        for d in far:
            go(wcopy(wg_send, wg_recv.at[z], nz + n_col + 4 + d, rid(0, d)))

    def gathered():
        for d in far:
            src = (z - d + nz) % nz
            wcopy(wg_send, wg_recv.at[src], nz + n_col + 4 + d, rid(0, -d)).wait_recv()
        for c in range(nz):
            gw_ref[c * chunk : (c + 1) * chunk, :] = wg_recv[c].astype(F32)

    order = [(1, 3), (1, -3), (1, 4), (1, 2), (1, -2), (1, 1), (1, -1), (0, 3), (0, -3), (0, 4)]
    order += [(1, 0), (0, 1), (0, -1), (0, 2), (0, -2), (0, 0)]

    def sib_copy(a, dz):
        k = a * nz + dz % nz
        return send(sib_send.at[k], sib_recv.at[k], sr_ss.at[k], sr_rs.at[k], sibling)

    for a, dz in order:
        for t in (0, 1):
            sib_send[a * nz + dz % nz, t] = total(5, 2 * rid(a, dz, 1) + t).astype(BF16)
        go(sib_copy(a, dz))
    over_z_done()

    def comb(a, dz, t):
        return total(5, 2 * rid(a, dz) + t) + sib_recv[a * nz + dz % nz, t].astype(F32)

    slots = {}
    for a in (0, 1):
        for e in signs:
            for name in ("three", "four", "one"):
                slots[name, a, e] = len(slots)
    for e in signs:
        slots["cross", 0, e] = len(slots)
        slots["two", 0, e] = len(slots)
    slots["zero", 0, 1] = len(slots)

    def ring(name, a, e, t, to):
        k = slots[name, a, e]
        return send(
            ring_send.at[k, pl.ds(t, 1)],
            ring_recv.at[k, pl.ds(t, 1)],
            ring_ss.at[2 * k + t],
            ring_rs.at[2 * k + t],
            to,
        )

    def ring_go(name, a, e, t, to, value):
        ring_send[slots[name, a, e], t] = value.astype(BF16)
        go(ring(name, a, e, t, to))

    def arrived(name, a, e, t):
        ring(name, a, e, t, across).wait_recv()
        return ring_recv[slots[name, a, e], t].astype(F32)

    for a in (1,):
        for e in signs:
            sib_copy(a, 3 * e).wait_recv()
            for t in (0, 1):
                ring_go("three", a, e, t, rid(0, e), comb(a, 3 * e, t))
        sib_copy(a, 4).wait_recv()
        for t, e in enumerate((-1, 1)):
            ring_go("four", a, e, t, rid(0, 2 * e), comb(a, 4, t))
    for a in (1,):
        for e in signs:
            sib_copy(a, e).wait_recv()
            for t in (0, 1):
                ring_go("one", a, e, t, rid(0, e), comb(a, e, t))
    for a in (0,):
        for e in signs:
            sib_copy(a, 3 * e).wait_recv()
            for t in (0, 1):
                ring_go("three", a, e, t, rid(0, e), comb(a, 3 * e, t))
        sib_copy(a, 4).wait_recv()
        for t, e in enumerate((-1, 1)):
            ring_go("four", a, e, t, rid(0, 2 * e), comb(a, 4, t))
    for a in (0,):
        for e in signs:
            sib_copy(a, e).wait_recv()
            for t in (0, 1):
                ring_go("one", a, e, t, rid(0, e), comb(a, e, t))

    drain(24)

    def near(a, e, t):
        value = comb(a, 2 * e, t) + arrived("three", a, e, t)
        if t == (0 if e == -1 else 1):
            value = value + arrived("four", a, e, t)
        return value

    for e in signs:
        sib_copy(1, 2 * e).wait_recv()
    for t in (0, 1):
        for e in signs:
            ring_go("cross", 0, e, t, across, near(1, e, t))
    over_col_done()
    sib_copy(1, 0).wait_recv()
    for t in (0, 1):
        value = comb(1, 0, t) + arrived("one", 1, 1, t) + arrived("one", 1, -1, t)
        ring_go("zero", 0, 1, t, across, value)
    for e in signs:
        sib_copy(0, 2 * e).wait_recv()
    for t in (0, 1):
        for e in signs:
            value = near(0, e, t) + arrived("cross", 0, e, t)
            ring_go("two", 0, e, t, rid(0, 2 * e), value)
    over_quad_done()
    drain(2 * len(signs) + len(far))
    sib_copy(0, 0).wait_recv()
    for t in (0, 1):
        value = comb(0, 0, t)
        for e in signs:
            value = value + arrived("one", 0, e, t)
        value = value + arrived("zero", 0, 1, t)
        for e in signs:
            value = value + arrived("two", 0, e, t)
        gf_ref[t * SIDE : (t + 1) * SIDE, :] = value.T.astype(BF16)
    gathered()
    drain(0)


def write_out(*refs):
    copies = [pltpu.make_async_copy(refs[i], refs[4 + i], refs[8].at[i]) for i in range(4)]
    for copy in copies:
        copy.start()
    for copy in copies:
        copy.wait()


def local(n_row, n_col, features, weight, bias, tile_values, tile_row, tile_col, tile_count, cotangent):
    nodes, f = features.shape
    h = weight.shape[1]
    cap = tile_values.shape[2]
    nz = n_row // 4
    chunk = f // nz
    scale = (n_row * n_col * nodes) ** (-0.5)
    pad = SIDE - tile_row.shape[-1]
    trow = jnp.pad(tile_row.reshape(1, -1), ((0, 0), (0, pad)))
    tcol = jnp.pad(tile_col.reshape(1, -1), ((0, 0), (0, pad)))
    vmem = pl.BlockSpec(memory_space=pltpu.VMEM)
    hbm = pl.BlockSpec(memory_space=pltpu.HBM)
    dma = pltpu.SemaphoreType.DMA
    square = (SIDE, SIDE)
    output, gf, gw, gb = pl.pallas_call(
        functools.partial(kernel, n_row, n_col, scale),
        out_shape=(
            jax.ShapeDtypeStruct((nodes, h), BF16),
            jax.ShapeDtypeStruct((nodes, f), BF16),
            jax.ShapeDtypeStruct((f, h), F32),
            jax.ShapeDtypeStruct((1, h), F32),
        ),
        in_specs=[hbm] * 6 + [pl.BlockSpec(memory_space=pltpu.SMEM), hbm],
        out_specs=(vmem,) * 4,
        scratch_shapes=[
            pltpu.VMEM((f, h), BF16),
            pltpu.VMEM((1, h), F32),
            pltpu.VMEM((1, SIDE), jnp.int32),
            pltpu.VMEM((1, SIDE), jnp.int32),
            pltpu.VMEM((2 * n_row,) + square, BF16),
            pltpu.VMEM((cap,) + square, BF16),
            pltpu.VMEM((nodes, h), BF16),
            pltpu.VMEM((16, SIDE), jnp.int32),
            pltpu.SMEM((16, SIDE), jnp.int32),
            pltpu.VMEM((cap,) + square, F32),
            pltpu.VMEM((2 * n_col,) + square, BF16),
            pltpu.VMEM((2 * n_col,) + square, BF16),
            pltpu.VMEM((2 * n_col,) + square, BF16),
            pltpu.VMEM((2 * nz, 2) + square, BF16),
            pltpu.VMEM((2 * nz, 2) + square, BF16),
            pltpu.VMEM((17, 2) + square, BF16),
            pltpu.VMEM((17, 2) + square, BF16),
            pltpu.VMEM((nz, chunk + 8, h), F32),
            pltpu.VMEM((nz, chunk + 8, h), F32),
            pltpu.VMEM((chunk + 8, h), F32),
            pltpu.VMEM((n_col, chunk + 8, h), F32),
            pltpu.VMEM((chunk + 16, h), BF16),
            pltpu.VMEM((4, chunk + 16, h), BF16),
            pltpu.VMEM((chunk, h), BF16),
            pltpu.VMEM((nz, chunk, h), BF16),
            dma((8,)),
            dma((4 * nz,)),
            dma((4 * nz,)),
            dma((2 * nz,)),
            dma((2 * nz,)),
            dma((4 * n_col,)),
            dma((4 * n_col,)),
            dma((2 * nz,)),
            dma((2 * nz,)),
            dma((34,)),
            dma((34,)),
            dma((2 * nz + n_col + 4,)),
            dma((2 * nz + n_col + 4,)),
        ],
        compiler_params=pltpu.CompilerParams(
            collective_id=0, has_side_effects=True, vmem_limit_bytes=48 * 1024 * 1024
        ),
    )(
        *(
            pltpu.with_memory_space_constraint(operand, pltpu.HBM)
            for operand in (
                features.reshape(2, SIDE, f),
                weight,
                bias.reshape(1, h),
                tile_values.reshape(tile_values.shape[2:]),
                trow,
                tcol,
            )
        ),
        tile_count,
        pltpu.with_memory_space_constraint(cotangent, pltpu.HBM),
    )
    results = (output, gf, gw, gb)
    output, gf, gw, gb = pl.pallas_call(
        write_out,
        out_shape=tuple(jax.ShapeDtypeStruct(a.shape, a.dtype) for a in results),
        in_specs=[pl.BlockSpec(memory_space=pl.ANY)] * 4,
        out_specs=(hbm,) * 4,
        scratch_shapes=[dma((4,))],
        compiler_params=pltpu.CompilerParams(vmem_limit_bytes=1024 * 1024),
    )(*(pltpu.with_memory_space_constraint(a, pltpu.VMEM) for a in results))
    return output, gf, gw, gb.reshape(h)


def solution(mesh):
    placed = (
        P(("col", "row"), None),
        P(),
        P(),
        P("row", "col", None, None, None),
        P("row", "col", None),
        P("row", "col", None),
        P("row", "col"),
        P(("row", "col"), None),
    )
    return jax.shard_map(
        functools.partial(local, mesh.shape["row"], mesh.shape["col"]),
        mesh=mesh,
        in_specs=placed,
        out_specs=(P(("row", "col"), None), P(("col", "row"), None), P(), P()),
        check_vma=False,
    )
```
